256 devices in a mesh: row: 32 (over x_lo, z, core), col: 8 (over x_hi, y).
Axes of the slice: x: 4 (x_hi: 2, x_lo: 2; x = x_hi * 2 + x_lo), y: 4, z: 8, core: 2. Of those that a mesh axis runs over, the one named last changes fastest.
Arguments:
- candidates: float32 [32, 4096], P(None, 'col'), may hold values from -1.5 to 1.5
- train_pts: float32 [32, 1024], P(None, 'col'), may hold values from -1.5 to 1.5
- length_rates: float32 [32], replicated, may hold values from 0.2 to 2
- kriging_weights: float32 [1024], P('col'), may hold values from -3 to 3
- component: int32 [1024], P('col'), may hold values from 0 to 32
- prior_var: float32 [4096], P('col'), may hold values from 60 to 90
- factor_panel: bfloat16 [1024, 98304], P(None, 'row'), may hold values from -0.0390625 to 0.0390625
- earlier_solution: bfloat16 [98304, 4096], P('row', 'col'), may hold values from -0.3984375 to 0.3984375
- diag_inverse: bfloat16 [2, 512, 512], replicated, may hold values from -4 to 4, as said below
- coupling: bfloat16 [512, 512], replicated, may hold values from -0.25 to 0.25
Outputs:
- post_mean: float32 [4096], P('col')
- variance: float32 [4096], P('col')
- gradient: float32 [32, 4096], P(None, 'col')
The draws below stay inside these ranges and needn't reach their ends.
Inputs may be any that keep to these rules, and one draw needn't show every extreme that they name: `diag_inverse`: each of the two blocks is lower triangular with a positive diagonal.
All inputs are finite; a program needn't handle non-finite values.
Results may differ from the reference program's by a relative error of at most 0.00035.
Values may be sent and summed in bfloat16 or wider, within the bound.
A program may use at most 64 MiB of HBM per device.

```python
import math
import jax
import jax.numpy as jnp
from jax import lax

DIM = 32
BLK = 512
WIN = 1024
CANDS = 4096
PREV = 98304


def draw_diag_inverse(key, part):
    first_key, second_key = jax.random.split(key)
    diagonal = jnp.exp(jax.random.uniform(first_key, (2, BLK), jnp.float32, math.log(0.25), 0.0))
    lower_part = jnp.clip(jax.random.normal(second_key, (2, BLK, BLK), jnp.float32), -4.0, 4.0) * (0.25 / math.sqrt(BLK))
    row_ids = jnp.arange(BLK)[:, None]
    col_ids = jnp.arange(BLK)[None, :]
    below = jnp.where(col_ids < row_ids, lower_part, 0.0)
    return (below + jnp.where(col_ids == row_ids, diagonal[:, :, None], 0.0)).astype(jnp.bfloat16)


def touch_ends(result, stream_key, least, high):
    dims = result.shape
    index_at = [jax.random.randint(jax.random.fold_in(stream_key, axis), (), 0, dims[axis]) for axis in range(len(dims))]
    result = result.at[tuple(index_at)].set(least)
    longest = dims.index(max(dims))
    index_at[longest] = (index_at[longest] + 1) % dims[longest]
    return result.at[tuple(index_at)].set(high)


def spiked(array, rng, source, target, shards_of, factor):
    def block_of(dim):
        return (jnp.arange(array.shape[dim]) // (array.shape[dim] // shards_of)).reshape((-1,) + (1,) * (array.ndim - 1 - dim))

    first = jax.random.permutation(rng, shards_of)[block_of(target)]
    second = (block_of(target) + shards_of // 2) % shards_of
    return jnp.where((block_of(source) == first) | (block_of(source) == second), factor * array, array)


def level_of(stream_key, dims, cuts, least, high):
    def one(position, shards_of):
        heights = jax.random.uniform(jax.random.fold_in(jax.random.fold_in(stream_key, 6), position), (shards_of,), jnp.float32, least / len(cuts), high / len(cuts))
        return jnp.repeat(jnp.exp(heights), dims[position] // shards_of).reshape((-1,) + (1,) * (len(dims) - position - 1))

    factor_of = one(*cuts[0])
    for cut in cuts[1:]:
        factor_of = factor_of * one(*cut)
    return factor_of


def noise(rng, shape, width, bound, pieces=(), kind=jnp.bfloat16):
    entries = width * jax.random.normal(rng, shape, jnp.float32)
    if pieces:
        entries = entries * level_of(rng, shape, pieces, -0.22, 0.18)
    return jnp.clip(entries, -bound, bound).astype(kind)


def noise_with(own_key, shape, scale, limit, cuts, heavy, held_as=jnp.bfloat16):
    result = scale * jax.random.normal(own_key, shape, jnp.float32)
    if cuts:
        result = result * level_of(own_key, shape, cuts, -0.22, 0.18)
    return jnp.clip(spiked(result, jax.random.fold_in(own_key, 3), *heavy), -limit, limit).astype(held_as)


def setup_inputs(seed: int = 0) -> dict:
    keys = jax.random.split(jax.random.key(seed), 11)
    candidates = noise(keys[0], (DIM, CANDS), 0.25, 1.5, ((1, 8),), jnp.float32)
    train_pts = noise(keys[1], (DIM, WIN), 0.25, 1.5, ((1, 8),), jnp.float32)
    length_rates = jnp.clip(jnp.exp(jax.random.uniform(keys[2], (DIM,), jnp.float32, math.log(0.2), math.log(2.0))), 0.2, 2.0)
    kriging_weights = noise(keys[3], (WIN,), 0.5, 3.0, ((0, 8),), jnp.float32)
    component = touch_ends(jax.random.randint(keys[4], (WIN,), 0, DIM + 1), jax.random.fold_in(keys[4], 1), 0, DIM).astype(jnp.int32)
    prior_var = jnp.clip(60.0 + 30.0 * jax.random.uniform(keys[5], (CANDS,), jnp.float32) ** level_of(keys[5], (CANDS,), ((0, 8),), -0.2, 0.2), 60.0, 90.0)
    factor_panel = noise_with(keys[6], (WIN, PREV), PREV ** -0.5, 0.0390625, ((1, 32),), (1, 0, 32, 2.75))
    earlier_solution = noise(keys[7], (PREV, CANDS), 0.1, 0.3984375, ((0, 32), (1, 8)))
    diag_inverse = draw_diag_inverse(jax.random.fold_in(keys[10], 71), 0)
    coupling = noise(keys[9], (BLK, BLK), BLK ** -0.5, 0.25)
    return dict(candidates=candidates, train_pts=train_pts, length_rates=length_rates, kriging_weights=kriging_weights, component=component, prior_var=prior_var, factor_panel=factor_panel, earlier_solution=earlier_solution, diag_inverse=diag_inverse, coupling=coupling)


def assemble(candidates, train_pts, length_rates, component):
    highest = lax.Precision.HIGHEST
    scaled = train_pts * length_rates[:, None]
    inner_prod = jnp.dot(scaled.T, candidates, precision=highest, preferred_element_type=jnp.float32)
    train_norm = jnp.sum(scaled * train_pts, axis=0)
    cand_norm = jnp.sum(length_rates[:, None] * candidates * candidates, axis=0)
    distance = train_norm[:, None] + cand_norm[None, :] - 2.0 * inner_prod
    kernel = jnp.exp(-0.5 * distance)
    levels = jnp.arange(1, candidates.shape[0] + 1, dtype=jnp.int32)
    selector = jnp.where(component[:, None] == levels[None, :], length_rates[None, :], jnp.float32(0.0))
    is_value = jnp.where(component == 0, jnp.float32(1.0), jnp.float32(0.0))
    along = jnp.dot(selector, candidates, precision=highest, preferred_element_type=jnp.float32)
    along = along - jnp.sum(selector * train_pts.T, axis=1)[:, None]
    cross_kernel = kernel * (is_value[:, None] + along)
    return kernel, selector, cross_kernel


def reference(candidates, train_pts, length_rates, kriging_weights, component, prior_var, factor_panel, earlier_solution, diag_inverse, coupling):
    highest = lax.Precision.HIGHEST
    kernel, selector, cross_kernel = assemble(candidates, train_pts, length_rates, component)
    update = jnp.dot(factor_panel, earlier_solution, preferred_element_type=jnp.float32)
    residual = (cross_kernel - update).astype(jnp.bfloat16)
    block_one = jnp.dot(diag_inverse[0], residual[:BLK], preferred_element_type=jnp.float32).astype(jnp.bfloat16)
    block_two_rhs = (residual[BLK:].astype(jnp.float32) - jnp.dot(coupling, block_one, preferred_element_type=jnp.float32)).astype(jnp.bfloat16)
    block_two = jnp.dot(diag_inverse[1], block_two_rhs, preferred_element_type=jnp.float32).astype(jnp.bfloat16)
    solved = jnp.concatenate([block_one, block_two], axis=0).astype(jnp.float32)
    variance = prior_var - jnp.sum(solved * solved, axis=0)
    weighted = kriging_weights[:, None] * cross_kernel
    post_mean = jnp.sum(weighted, axis=0)
    sel_sum = jnp.dot((selector * kriging_weights[:, None]).T, kernel, precision=highest, preferred_element_type=jnp.float32)
    pts_sum = jnp.dot(train_pts, weighted, precision=highest, preferred_element_type=jnp.float32)
    gradient = sel_sum - length_rates[:, None] * (candidates * post_mean[None, :] - pts_sum)
    return post_mean, variance, gradient
```

```python
import jax
import jax.numpy as jnp
from jax import lax
from jax.experimental import pallas as pl
from jax.experimental.pallas import tpu as pltpu
from jax.sharding import PartitionSpec as P

MESH = pl.DeviceIdType.MESH
F32 = jnp.float32
BF16 = jnp.bfloat16
HIGHEST = lax.Precision.HIGHEST
NT = (((1,), (1,)), ((), ()))
TN = (((0,), (0,)), ((), ()))

ROWS = 1024
CAND = 512
DEPTH = 3072
DIM = 32
CHUNKS = 4
STEP = ROWS // CHUNKS
HALF = CAND // 2
QUARTER = CAND // 4
OWN = CAND // 32
ZS = 8
BPARTS = 4


def remote(src, dst, send_sem, recv_sem, **where):
    return pltpu.make_async_remote_copy(
        src_ref=src,
        dst_ref=dst,
        send_sem=send_sem,
        recv_sem=recv_sem,
        device_id=where,
        device_id_type=MESH,
    )


def exact(a, b, dims=(((1,), (0,)), ((), ()))):
    return lax.dot_general(a, b, dims, precision=HIGHEST, preferred_element_type=F32)


def kernel(
    cand_hbm,
    points_hbm,
    rates_hbm,
    weights_hbm,
    component_hbm,
    prior_hbm,
    panel_hbm,
    earlier_hbm,
    diag_hbm,
    coupling_hbm,
    mean_ref,
    variance_ref,
    gradient_ref,
    panel,
    earlier,
    diag,
    coupling,
    cand,
    rates,
    prior,
    component,
    pack,
    packs,
    cand_t,
    part,
    core_in,
    pair,
    pair_in,
    plane,
    z_in,
    own_cross,
    sums,
    panel_sem,
    earlier_sem,
    small_sem,
    pack_send,
    pack_recv,
    core_send,
    core_recv,
    pair_send,
    pair_recv,
    z_send,
    z_recv,
    sums_send,
    sums_recv,
):
    row = lax.axis_index("row")
    col = lax.axis_index("col")
    core = lax.rem(row, 2)
    z = lax.rem(row // 2, ZS)
    x = row // (2 * ZS)

    def row_at(x_at, z_at, core_at):
        return (x_at * ZS + z_at) * 2 + core_at

    half = lax.rem(core + x + z // 4, 2)
    place = (half * 2 + x) * ZS + z

    barrier = pltpu.get_barrier_semaphore()

    def greet_row(i, carry):
        pl.semaphore_signal(
            barrier, inc=1, device_id={"row": lax.rem(row + i, 4 * ZS)}, device_id_type=MESH
        )
        return carry

    def greet_col(i, carry):
        pl.semaphore_signal(
            barrier, inc=1, device_id={"col": lax.rem(col + i, 8)}, device_id_type=MESH
        )
        return carry

    panel_in = [
        pltpu.make_async_copy(
            panel_hbm.at[pl.ds(c * STEP, STEP)], panel.at[pl.ds(c * STEP, STEP)], panel_sem.at[c]
        )
        for c in range(CHUNKS)
    ]
    deep = DEPTH // BPARTS
    earlier_in = [
        pltpu.make_async_copy(
            earlier_hbm.at[pl.ds(i * deep, deep)], earlier.at[pl.ds(i * deep, deep)], earlier_sem.at[i]
        )
        for i in range(BPARTS)
    ]
    small_in = [
        pltpu.make_async_copy(points_hbm, pack.at[pl.ds(0, DIM)], small_sem.at[0]),
        pltpu.make_async_copy(weights_hbm, pack.at[pl.ds(DIM, 1)], small_sem.at[1]),
        pltpu.make_async_copy(component_hbm, component, small_sem.at[2]),
        pltpu.make_async_copy(cand_hbm, cand, small_sem.at[3]),
        pltpu.make_async_copy(rates_hbm, rates, small_sem.at[4]),
        pltpu.make_async_copy(prior_hbm, prior, small_sem.at[5]),
        pltpu.make_async_copy(diag_hbm, diag, small_sem.at[6]),
        pltpu.make_async_copy(coupling_hbm, coupling, small_sem.at[7]),
    ]
    panel_in[0].start()
    for copy in earlier_in:
        copy.start()
    panel_in[1].start()
    for copy in small_in[:6]:
        copy.start()
    lax.fori_loop(1, 4 * ZS, greet_row, 0)
    lax.fori_loop(1, 8, greet_col, 0)
    panel_in[0].wait()
    for copy in earlier_in:
        copy.wait()
    for copy in panel_in[2:]:
        copy.start()
    for copy in small_in[6:]:
        copy.start()

    def multiply(c, which):
        product = jnp.dot(
            panel[pl.ds(c * STEP, STEP)],
            earlier[:, pl.ds(pl.multiple_of(which * HALF, HALF), HALF)],
            preferred_element_type=F32,
        )
        part[
            pl.ds(pl.multiple_of(which * HALF, HALF), HALF), pl.ds(c * STEP, STEP)
        ] = product.astype(BF16).T

    def rows_of(c):
        return pl.ds(c * STEP, STEP)

    core_copies = [
        remote(
            part.at[pl.ds(pl.multiple_of((1 - half) * HALF, HALF), HALF), rows_of(c)],
            core_in.at[:, rows_of(c)],
            core_send.at[c],
            core_recv.at[c],
            row=row_at(x, z, 1 - core),
        )
        for c in range(CHUNKS)
    ]
    pair_copies = [
        remote(
            pair.at[pl.ds(pl.multiple_of((1 - x) * QUARTER, QUARTER), QUARTER), rows_of(c)],
            pair_in.at[:, rows_of(c)],
            pair_send.at[c],
            pair_recv.at[c],
            row=row_at(1 - x, z, 1 - core),
        )
        for c in range(CHUNKS)
    ]

    def core_sum(c):
        core_copies[c].wait_recv()
        mine = part[pl.ds(pl.multiple_of(half * HALF, HALF), HALF), rows_of(c)].astype(F32)
        pair[:, rows_of(c)] = (mine + core_in[:, rows_of(c)].astype(F32)).astype(BF16)
        pair_copies[c].start()

    def z_order(i):
        return (4, 3, 5, 2, 6, 1, 7)[i]

    def pair_sum(c):
        pair_copies[c].wait_recv()
        mine = pair[pl.ds(pl.multiple_of(x * QUARTER, QUARTER), QUARTER), rows_of(c)].astype(F32)
        plane[:, rows_of(c)] = (mine + pair_in[:, rows_of(c)].astype(F32)).astype(BF16)
        for i in range(ZS - 1):
            other = lax.rem(z + z_order(i), ZS)
            other_core = lax.rem(half + x + other // 4, 2)
            remote(
                plane.at[pl.ds(pl.multiple_of(other * OWN, OWN), OWN), rows_of(c)],
                z_in.at[i, :, rows_of(c)],
                z_send.at[c],
                z_recv.at[c],
                row=row_at(x, other, other_core),
            ).start()

    for c in range(CHUNKS):
        if c:
            panel_in[c].wait()
        multiply(c, 1 - half)
        if c == 0:
            for copy in small_in[:6]:
                copy.wait()
            pack[pl.ds(DIM + 1, 7)] = jnp.zeros((7, 128), F32)
            pack[pl.ds(DIM + 1, 1)] = component[...].astype(F32)
            packs[pl.ds(col, 1)] = pack[...][None]
            pl.semaphore_wait(barrier, 4 * ZS - 1 + 7)
        core_copies[c].start()
        if c == 0:

            def give_pack(i, carry):
                remote(
                    pack, packs.at[col], pack_send, pack_recv, col=lax.rem(col + i, 8)
                ).start()
                return carry

            lax.fori_loop(1, 8, give_pack, 0)
        multiply(c, half)
        if c:
            core_sum(c - 1)
    core_sum(CHUNKS - 1)

    packs_moved = remote(
        packs.at[pl.ds(0, 7)], packs.at[pl.ds(0, 7)], pack_send, pack_recv, col=col
    )
    packs_moved.wait_recv()
    lane = lax.broadcasted_iota(jnp.int32, (DIM, DIM), 1)
    level = lax.broadcasted_iota(jnp.int32, (DIM, DIM), 0)
    rate = jnp.sum(jnp.where(lane == level, rates[...], 0.0), axis=1, keepdims=True)
    points = jnp.concatenate([packs[j, :DIM] for j in range(8)], axis=1)
    weights = jnp.concatenate([packs[j, DIM : DIM + 1] for j in range(8)], axis=1)
    kinds = jnp.concatenate([packs[j, DIM + 1 : DIM + 2] for j in range(8)], axis=1)
    scaled = points * rate
    point_norm = jnp.sum(scaled * points, axis=0, keepdims=True)
    levels = lax.broadcasted_iota(jnp.int32, (DIM, ROWS), 0) + 1
    selector = jnp.where(kinds == levels.astype(F32), rate, 0.0)
    offset = jnp.where(kinds == 0.0, 1.0, 0.0) - jnp.sum(selector * points, axis=0, keepdims=True)
    cand_t[...] = cand[...].T

    def assemble(some):
        norm = jnp.sum(some * some * rates[...], axis=1, keepdims=True)
        distance = point_norm + norm - 2.0 * exact(some, scaled)
        near = jnp.exp(-0.5 * distance)
        return near, near * (offset + exact(some, selector))

    own_cross[...] = assemble(cand_t[pl.ds(pl.multiple_of(place * OWN, OWN), OWN)])[1]

    for c in range(CHUNKS):
        pair_sum(c)

    def residual(c):
        remote(
            z_in.at[:, :, rows_of(c)], z_in.at[:, :, rows_of(c)], z_send.at[c], z_recv.at[c], row=row
        ).wait_recv()
        total = plane[pl.ds(pl.multiple_of(z * OWN, OWN), OWN), rows_of(c)].astype(F32)
        for i in range(ZS - 1):
            total += z_in[i, :, rows_of(c)].astype(F32)
        return (own_cross[:, rows_of(c)] - total).astype(BF16)

    def nt(a, b):
        return lax.dot_general(a, b, NT, preferred_element_type=F32)

    small_in[6].wait()
    small_in[7].wait()
    first_rhs = jnp.concatenate([residual(0), residual(1)], axis=1)
    block_one = nt(first_rhs, diag[0]).astype(BF16)
    coupled = nt(block_one, coupling[...])
    one = block_one.astype(F32)
    squares = jnp.sum(one * one, axis=1, keepdims=True)
    second = jnp.concatenate([residual(2), residual(3)], axis=1)
    second_rhs = (second.astype(F32) - coupled).astype(BF16)
    two = nt(second_rhs, diag[1]).astype(BF16).astype(F32)
    squares += jnp.sum(two * two, axis=1, keepdims=True)
    lane = lax.broadcasted_iota(jnp.int32, (OWN, QUARTER), 1)
    number = lax.broadcasted_iota(jnp.int32, (OWN, QUARTER), 0)
    sums[pl.ds(place, 1)] = jnp.sum(
        jnp.where(lane == number + z * OWN, squares, 0.0), axis=0, keepdims=True
    )

    def give_sums(i, carry):
        turn = i // 4
        odd = lax.rem(turn, 2)
        ahead = odd * (4 - (turn + 1) // 2) + (1 - odd) * (4 + turn // 2)
        other = lax.rem(z + ahead, ZS)
        other_x = lax.rem(x + 1 + (lax.rem(i, 4) // 2), 2)
        other_core = lax.rem(core + 1 + lax.rem(i, 2), 2)
        remote(
            sums.at[pl.ds(place, 1)],
            sums.at[pl.ds(place, 1)],
            sums_send,
            sums_recv,
            row=row_at(other_x, other, other_core),
        ).start()
        return carry

    lax.fori_loop(0, 4 * ZS - 1, give_sums, 0)

    near, cross = assemble(cand_t[...])
    weighted = cross * weights
    mean = jnp.sum(weighted, axis=1, keepdims=True)
    from_selector = exact(near, selector * weights, NT)
    from_points = exact(weighted, points, NT)
    gradient = from_selector - rates[...] * (cand_t[...] * mean - from_points)
    gradient_ref[...] = gradient.T
    mean_ref[...] = jnp.broadcast_to(mean, (CAND, 128)).T[:1]

    remote(
        sums.at[pl.ds(0, 4 * ZS - 1)], sums.at[pl.ds(0, 4 * ZS - 1)], sums_send, sums_recv, row=row
    ).wait()
    for q in range(4):
        variance_ref[:, pl.ds(q * QUARTER, QUARTER)] = prior[
            :, pl.ds(q * QUARTER, QUARTER)
        ] - jnp.sum(sums[pl.ds(q * ZS, ZS)], axis=0, keepdims=True)

    packs_moved.wait_send()
    for c in range(CHUNKS):
        core_copies[c].wait_send()
        pair_copies[c].wait_send()
        remote(
            z_in.at[:, :, rows_of(c)], z_in.at[:, :, rows_of(c)], z_send.at[c], z_recv.at[c], row=row
        ).wait_send()


def shards(
    candidates,
    train_pts,
    length_rates,
    kriging_weights,
    component,
    prior_var,
    factor_panel,
    earlier_solution,
    diag_inverse,
    coupling,
):
    dma = pltpu.SemaphoreType.DMA
    mean, variance, gradient = pl.pallas_call(
        kernel,
        out_shape=(
            jax.ShapeDtypeStruct((1, CAND), F32),
            jax.ShapeDtypeStruct((1, CAND), F32),
            jax.ShapeDtypeStruct((DIM, CAND), F32),
        ),
        in_specs=[pl.BlockSpec(memory_space=pltpu.HBM)] * 10,
        out_specs=[pl.BlockSpec(memory_space=pltpu.VMEM)] * 3,
        scratch_shapes=[
            pltpu.VMEM((ROWS, DEPTH), BF16),
            pltpu.VMEM((DEPTH, CAND), BF16),
            pltpu.VMEM((2, 512, 512), BF16),
            pltpu.VMEM((512, 512), BF16),
            pltpu.VMEM((DIM, CAND), F32),
            pltpu.VMEM((1, DIM), F32),
            pltpu.VMEM((1, CAND), F32),
            pltpu.VMEM((1, 128), jnp.int32),
            pltpu.VMEM((DIM + 8, 128), F32),
            pltpu.VMEM((8, DIM + 8, 128), F32),
            pltpu.VMEM((CAND, DIM), F32),
            pltpu.VMEM((CAND, ROWS), BF16),
            pltpu.VMEM((HALF, ROWS), BF16),
            pltpu.VMEM((HALF, ROWS), BF16),
            pltpu.VMEM((QUARTER, ROWS), BF16),
            pltpu.VMEM((QUARTER, ROWS), BF16),
            pltpu.VMEM((ZS - 1, OWN, ROWS), BF16),
            pltpu.VMEM((OWN, ROWS), F32),
            pltpu.VMEM((4 * ZS, 128), F32),
            dma((CHUNKS,)),
            dma((BPARTS,)),
            dma((8,)),
            dma,
            dma,
            dma((CHUNKS,)),
            dma((CHUNKS,)),
            dma((CHUNKS,)),
            dma((CHUNKS,)),
            dma((CHUNKS,)),
            dma((CHUNKS,)),
            dma,
            dma,
        ],
        compiler_params=pltpu.CompilerParams(
            collective_id=0, has_side_effects=True, vmem_limit_bytes=56 << 20
        ),
    )(
        candidates,
        train_pts,
        length_rates.reshape(1, DIM),
        kriging_weights.reshape(1, -1),
        component.reshape(1, -1),
        prior_var.reshape(1, CAND),
        factor_panel,
        earlier_solution,
        diag_inverse,
        coupling,
    )
    return mean.reshape(CAND), variance.reshape(CAND), gradient


def solution(mesh):
    return jax.shard_map(
        shards,
        mesh=mesh,
        in_specs=(
            P(None, "col"),
            P(None, "col"),
            P(),
            P("col"),
            P("col"),
            P("col"),
            P(None, "row"),
            P("row", "col"),
            P(),
            P(),
        ),
        out_specs=(P("col"), P("col"), P(None, "col")),
        check_vma=False,
    )
```

```python
import jax
import jax.numpy as jnp
from jax import lax
from jax.experimental import pallas as pl
from jax.experimental.pallas import tpu as pltpu
from jax.sharding import PartitionSpec as P

MESH = pl.DeviceIdType.MESH
F32 = jnp.float32
BF16 = jnp.bfloat16
NT = (((1,), (1,)), ((), ()))

ROWS = 1024
CAND = 512
DEPTH = 3072
DIM = 32
CHUNKS = 4
STEP = ROWS // CHUNKS
HALF = CAND // 2
QUARTER = CAND // 4
OWN = CAND // 32
ZS = 8
BPARTS = 4


def remote(src, dst, send_sem, recv_sem, **where):
    return pltpu.make_async_remote_copy(
        src_ref=src,
        dst_ref=dst,
        send_sem=send_sem,
        recv_sem=recv_sem,
        device_id=where,
        device_id_type=MESH,
    )


def split(value):
    one = value.astype(BF16)
    rest = value - one.astype(F32)
    two = rest.astype(BF16)
    return [one, two, (rest - two.astype(F32)).astype(BF16)]


def floats(terms):
    return [term.astype(F32) for term in terms]


def kernel(
    cand_hbm,
    points_hbm,
    rates_hbm,
    weights_hbm,
    component_hbm,
    prior_hbm,
    panel_hbm,
    earlier_hbm,
    diag_hbm,
    coupling_hbm,
    mean_ref,
    variance_ref,
    gradient_ref,
    panel,
    earlier,
    diag,
    coupling,
    cand,
    rates,
    prior,
    component,
    pack,
    packs,
    left,
    right,
    by_selector,
    by_points,
    part,
    core_in,
    pair,
    pair_in,
    plane,
    z_in,
    own_cross,
    sums,
    panel_sem,
    earlier_sem,
    small_sem,
    pack_send,
    pack_recv,
    core_send,
    core_recv,
    pair_send,
    pair_recv,
    z_send,
    z_recv,
    sums_send,
    sums_recv,
):
    row = lax.axis_index("row")
    col = lax.axis_index("col")
    core = lax.rem(row, 2)
    z = lax.rem(row // 2, ZS)
    x = row // (2 * ZS)

    def row_at(x_at, z_at, core_at):
        return (x_at * ZS + z_at) * 2 + core_at

    half = lax.rem(core + x + z // 4, 2)
    place = (half * 2 + x) * ZS + z

    barrier = pltpu.get_barrier_semaphore()

    def plane_at(i):
        other = lax.rem(z + i, ZS)
        return row_at(x, other, lax.rem(half + x + other // 4, 2))

    def greet_plane(i, carry):
        pl.semaphore_signal(barrier, inc=1, device_id={"row": plane_at(i)}, device_id_type=MESH)
        return carry

    def greet_col(i, carry):
        pl.semaphore_signal(
            barrier, inc=1, device_id={"col": lax.rem(col + i, 8)}, device_id_type=MESH
        )
        return carry

    panel_in = [
        pltpu.make_async_copy(
            panel_hbm.at[pl.ds(c * STEP, STEP)], panel.at[pl.ds(c * STEP, STEP)], panel_sem.at[c]
        )
        for c in range(CHUNKS)
    ]
    deep = DEPTH // BPARTS
    earlier_in = [
        pltpu.make_async_copy(
            earlier_hbm.at[pl.ds(i * deep, deep)], earlier.at[pl.ds(i * deep, deep)], earlier_sem.at[i]
        )
        for i in range(BPARTS)
    ]
    small_in = [
        pltpu.make_async_copy(points_hbm, pack.at[pl.ds(0, DIM)], small_sem.at[0]),
        pltpu.make_async_copy(weights_hbm, pack.at[pl.ds(DIM, 1)], small_sem.at[1]),
        pltpu.make_async_copy(component_hbm, component, small_sem.at[2]),
        pltpu.make_async_copy(cand_hbm, cand, small_sem.at[3]),
        pltpu.make_async_copy(rates_hbm, rates, small_sem.at[4]),
        pltpu.make_async_copy(prior_hbm, prior, small_sem.at[5]),
        pltpu.make_async_copy(diag_hbm, diag, small_sem.at[6]),
        pltpu.make_async_copy(coupling_hbm, coupling, small_sem.at[7]),
    ]
    panel_in[0].start()
    for copy in earlier_in:
        copy.start()
    panel_in[1].start()
    for copy in small_in[:6]:
        copy.start()
    lax.fori_loop(1, ZS, greet_plane, 0)
    lax.fori_loop(1, 8, greet_col, 0)
    for other in (row_at(x, z, 1 - core), row_at(1 - x, z, 1 - core)):
        pl.semaphore_signal(barrier, inc=1, device_id={"row": other}, device_id_type=MESH)
    panel_in[0].wait()
    for copy in earlier_in:
        copy.wait()
    for copy in panel_in[2:]:
        copy.start()
    for copy in small_in[6:]:
        copy.start()

    def rows_of(c):
        return pl.ds(c * STEP, STEP)

    core_copies = [
        remote(
            part.at[pl.ds(pl.multiple_of((1 - half) * HALF, HALF), HALF), rows_of(c)],
            core_in.at[:, rows_of(c)],
            core_send.at[c],
            core_recv.at[c],
            row=row_at(x, z, 1 - core),
        )
        for c in range(CHUNKS)
    ]
    pair_copies = [
        remote(
            pair.at[pl.ds(pl.multiple_of((1 - x) * QUARTER, QUARTER), QUARTER), rows_of(c)],
            pair_in.at[:, rows_of(c)],
            pair_send.at[c],
            pair_recv.at[c],
            row=row_at(1 - x, z, 1 - core),
        )
        for c in range(CHUNKS)
    ]

    def core_sum(c):
        core_copies[c].wait_recv()
        mine = part[pl.ds(pl.multiple_of(half * HALF, HALF), HALF), rows_of(c)].astype(F32)
        pair[:, rows_of(c)] = (mine + core_in[:, rows_of(c)].astype(F32)).astype(BF16)
        pair_copies[c].start()

    def z_order(i):
        return (4, 3, 5, 2, 6, 1, 7)[i]

    def pair_sum(c):
        pair_copies[c].wait_recv()
        mine = pair[pl.ds(pl.multiple_of(x * QUARTER, QUARTER), QUARTER), rows_of(c)].astype(F32)
        plane[:, rows_of(c)] = (mine + pair_in[:, rows_of(c)].astype(F32)).astype(BF16)
        for i in range(ZS - 1):
            other = lax.rem(z + z_order(i), ZS)
            remote(
                plane.at[pl.ds(pl.multiple_of(other * OWN, OWN), OWN), rows_of(c)],
                z_in.at[i, :, rows_of(c)],
                z_send.at[c],
                z_recv.at[c],
                row=plane_at(z_order(i)),
            ).start()

    for c in range(CHUNKS):
        if c:
            panel_in[c].wait()
        product = jnp.dot(panel[rows_of(c)], earlier[...], preferred_element_type=F32)
        part[:, rows_of(c)] = product.astype(BF16).T
        if c == 0:
            for copy in small_in[:6]:
                copy.wait()
            pack[pl.ds(DIM + 1, 7)] = jnp.zeros((7, 128), F32)
            pack[pl.ds(DIM + 1, 1)] = component[...].astype(F32)
            packs[pl.ds(col, 1)] = pack[...][None]
            pl.semaphore_wait(barrier, 7 + 7 + 2)
        core_copies[c].start()
        if c == 0:

            def give_pack(i, carry):
                remote(
                    pack, packs.at[col], pack_send, pack_recv, col=lax.rem(col + i, 8)
                ).start()
                return carry

            lax.fori_loop(1, 8, give_pack, 0)
        if c:
            core_sum(c - 1)
    core_sum(CHUNKS - 1)

    for c in range(CHUNKS):
        pair_sum(c)

    packs_moved = remote(
        packs.at[pl.ds(0, 7)], packs.at[pl.ds(0, 7)], pack_send, pack_recv, col=col
    )
    packs_moved.wait_recv()
    lane = lax.broadcasted_iota(jnp.int32, (DIM, DIM), 1)
    level = lax.broadcasted_iota(jnp.int32, (DIM, DIM), 0)
    rate = jnp.sum(jnp.where(lane == level, rates[...], 0.0), axis=1, keepdims=True)
    points = jnp.concatenate([packs[j, :DIM] for j in range(8)], axis=1)
    weights = jnp.concatenate([packs[j, DIM : DIM + 1] for j in range(8)], axis=1)
    kinds = jnp.concatenate([packs[j, DIM + 1 : DIM + 2] for j in range(8)], axis=1)
    scaled = points * rate
    levels = lax.broadcasted_iota(jnp.int32, (DIM, ROWS), 0)
    selector = jnp.where(kinds == (levels + 1).astype(F32), rate, 0.0)
    offset = jnp.where(kinds == 0.0, 1.0, 0.0) - jnp.sum(selector * points, axis=0, keepdims=True)
    point_norm = -0.5 * jnp.sum(scaled * points, axis=0, keepdims=True)
    spread = cand[...]
    cand_norm = -0.5 * jnp.sum(rate * spread * spread, axis=0, keepdims=True)

    def rows_in(shape, first, second):
        at = lax.broadcasted_iota(jnp.int32, shape, 0)
        result = jnp.zeros(shape, F32)
        for i, row_value in enumerate(first + second):
            result = jnp.where(at == i, row_value, result)
        return result.astype(BF16)

    def right_side(factor, first, second):
        one, two, three = split(factor)
        return jnp.concatenate(
            [one, two, one, three, two, one, rows_in((DIM, ROWS), first, second)], axis=0
        )

    ones = [1.0, 1.0, 1.0]
    right[:, :ROWS] = right_side(scaled, floats(split(point_norm)), ones)
    right[:, ROWS:] = right_side(selector, floats(split(offset)), [0.0, 0.0, 0.0])
    one, two, three = split(spread)
    left[:, : 7 * DIM] = jnp.concatenate(
        [one, one, two, one, two, three, rows_in((DIM, CAND), ones, floats(split(cand_norm)))],
        axis=0,
    ).T
    by_selector[...] = jnp.concatenate(split(selector * weights)[:2], axis=0)
    by_points[: 2 * DIM] = jnp.concatenate(split(points * weights)[:2], axis=0)
    by_points[2 * DIM :] = rows_in((DIM, ROWS), floats(split(weights)), [])

    def assemble(some):
        both = jnp.dot(some, right[...], preferred_element_type=F32)
        near = jnp.exp(both[:, :ROWS])
        return near, near * both[:, ROWS:]

    own_cross[...] = assemble(
        left[pl.ds(pl.multiple_of(place * OWN, OWN), OWN), : 7 * DIM]
    )[1]

    def residual(c):
        remote(
            z_in.at[:, :, rows_of(c)], z_in.at[:, :, rows_of(c)], z_send.at[c], z_recv.at[c], row=row
        ).wait_recv()
        total = plane[pl.ds(pl.multiple_of(z * OWN, OWN), OWN), rows_of(c)].astype(F32)
        for i in range(ZS - 1):
            total += z_in[i, :, rows_of(c)].astype(F32)
        return (own_cross[:, rows_of(c)] - total).astype(BF16)

    def nt(a, b):
        return lax.dot_general(a, b, NT, preferred_element_type=F32)

    small_in[6].wait()
    small_in[7].wait()
    first_rhs = jnp.concatenate([residual(0), residual(1)], axis=1)
    block_one = nt(first_rhs, diag[0]).astype(BF16)
    coupled = nt(block_one, coupling[...])
    one = block_one.astype(F32)
    squares = jnp.sum(one * one, axis=1, keepdims=True)
    second = jnp.concatenate([residual(2), residual(3)], axis=1)
    second_rhs = (second.astype(F32) - coupled).astype(BF16)
    two = nt(second_rhs, diag[1]).astype(BF16).astype(F32)
    squares += jnp.sum(two * two, axis=1, keepdims=True)
    lane = lax.broadcasted_iota(jnp.int32, (OWN, QUARTER), 1)
    number = lax.broadcasted_iota(jnp.int32, (OWN, QUARTER), 0)
    sums[pl.ds(place, 1)] = jnp.sum(
        jnp.where(lane == number + z * OWN, squares, 0.0), axis=0, keepdims=True
    )

    def give_sums(i, carry):
        turn = i // 4
        odd = lax.rem(turn, 2)
        ahead = odd * (4 - (turn + 1) // 2) + (1 - odd) * (4 + turn // 2)
        other = lax.rem(z + ahead, ZS)
        other_x = lax.rem(x + 1 + (lax.rem(i, 4) // 2), 2)
        other_core = lax.rem(core + 1 + lax.rem(i, 2), 2)
        remote(
            sums.at[pl.ds(place, 1)],
            sums.at[pl.ds(place, 1)],
            sums_send,
            sums_recv,
            row=row_at(other_x, other, other_core),
        ).start()
        return carry

    lax.fori_loop(0, 4 * ZS - 1, give_sums, 0)

    for q in range(4):
        some = pl.ds(q * QUARTER, QUARTER)
        near, cross = assemble(left[some, : 7 * DIM])
        near_one, near_two, _ = split(near)
        cross_one, cross_two, _ = split(cross)
        by_near = (nt(near_one, by_selector[...]) + nt(near_two, by_selector[...])).T
        by_cross = (nt(cross_one, by_points[...]) + nt(cross_two, by_points[...])).T
        mean = jnp.sum(by_cross[2 * DIM :], axis=0, keepdims=True)
        mean_ref[:, some] = mean
        gradient_ref[:, some] = (by_near[:DIM] + by_near[DIM:]) - rate * (
            cand[:, some] * mean - (by_cross[:DIM] + by_cross[DIM : 2 * DIM])
        )

    remote(
        sums.at[pl.ds(0, 4 * ZS - 1)], sums.at[pl.ds(0, 4 * ZS - 1)], sums_send, sums_recv, row=row
    ).wait()
    for q in range(4):
        variance_ref[:, pl.ds(q * QUARTER, QUARTER)] = prior[
            :, pl.ds(q * QUARTER, QUARTER)
        ] - jnp.sum(sums[pl.ds(q * ZS, ZS)], axis=0, keepdims=True)

    packs_moved.wait_send()
    for c in range(CHUNKS):
        core_copies[c].wait_send()
        pair_copies[c].wait_send()
        remote(
            z_in.at[:, :, rows_of(c)], z_in.at[:, :, rows_of(c)], z_send.at[c], z_recv.at[c], row=row
        ).wait_send()


def shards(
    candidates,
    train_pts,
    length_rates,
    kriging_weights,
    component,
    prior_var,
    factor_panel,
    earlier_solution,
    diag_inverse,
    coupling,
):
    dma = pltpu.SemaphoreType.DMA
    mean, variance, gradient = pl.pallas_call(
        kernel,
        out_shape=(
            jax.ShapeDtypeStruct((1, CAND), F32),
            jax.ShapeDtypeStruct((1, CAND), F32),
            jax.ShapeDtypeStruct((DIM, CAND), F32),
        ),
        in_specs=[pl.BlockSpec(memory_space=pltpu.HBM)] * 10,
        out_specs=[pl.BlockSpec(memory_space=pltpu.VMEM)] * 3,
        scratch_shapes=[
            pltpu.VMEM((ROWS, DEPTH), BF16),
            pltpu.VMEM((DEPTH, CAND), BF16),
            pltpu.VMEM((2, 512, 512), BF16),
            pltpu.VMEM((512, 512), BF16),
            pltpu.VMEM((DIM, CAND), F32),
            pltpu.VMEM((1, DIM), F32),
            pltpu.VMEM((1, CAND), F32),
            pltpu.VMEM((1, 128), jnp.int32),
            pltpu.VMEM((DIM + 8, 128), F32),
            pltpu.VMEM((8, DIM + 8, 128), F32),
            pltpu.VMEM((CAND, 8 * DIM), BF16),
            pltpu.VMEM((7 * DIM, 2 * ROWS), BF16),
            pltpu.VMEM((2 * DIM, ROWS), BF16),
            pltpu.VMEM((3 * DIM, ROWS), BF16),
            pltpu.VMEM((CAND, ROWS), BF16),
            pltpu.VMEM((HALF, ROWS), BF16),
            pltpu.VMEM((HALF, ROWS), BF16),
            pltpu.VMEM((QUARTER, ROWS), BF16),
            pltpu.VMEM((QUARTER, ROWS), BF16),
            pltpu.VMEM((ZS - 1, OWN, ROWS), BF16),
            pltpu.VMEM((OWN, ROWS), F32),
            pltpu.VMEM((4 * ZS, 128), F32),
            dma((CHUNKS,)),
            dma((BPARTS,)),
            dma((8,)),
            dma,
            dma,
            dma((CHUNKS,)),
            dma((CHUNKS,)),
            dma((CHUNKS,)),
            dma((CHUNKS,)),
            dma((CHUNKS,)),
            dma((CHUNKS,)),
            dma,
            dma,
        ],
        compiler_params=pltpu.CompilerParams(
            collective_id=0, has_side_effects=True, vmem_limit_bytes=56 << 20
        ),
    )(
        candidates,
        train_pts,
        length_rates.reshape(1, DIM),
        kriging_weights.reshape(1, -1),
        component.reshape(1, -1),
        prior_var.reshape(1, CAND),
        factor_panel,
        earlier_solution,
        diag_inverse,
        coupling,
    )
    return mean.reshape(CAND), variance.reshape(CAND), gradient


def solution(mesh):
    return jax.shard_map(
        shards,
        mesh=mesh,
        in_specs=(
            P(None, "col"),
            P(None, "col"),
            P(),
            P("col"),
            P("col"),
            P("col"),
            P(None, "row"),
            P("row", "col"),
            P(),
            P(),
        ),
        out_specs=(P("col"), P("col"), P(None, "col")),
        check_vma=False,
    )
```

```python
import jax
import jax.numpy as jnp
from jax import lax
from jax.experimental import pallas as pl
from jax.experimental.pallas import tpu as pltpu
from jax.sharding import PartitionSpec as P

MESH = pl.DeviceIdType.MESH
F32 = jnp.float32
BF16 = jnp.bfloat16
NT = (((1,), (1,)), ((), ()))

ROWS = 1024
CAND = 512
DEPTH = 3072
DIM = 32
PARTS = 2
SIZES = (256, 256, 256, 256)
KINDS = "baad"
ORDER = (1, 2, 0)
HALF = CAND // 2
QUARTER = CAND // 4
OWN = CAND // 32
ZS = 8
CHUNKS = len(SIZES)
STARTS = tuple(sum(SIZES[:c]) for c in range(CHUNKS))
TURNS = (4, 3, 5, 2, 6, 1, 7, 0)
BPARTS = 4


def remote(src, dst, send_sem, recv_sem, **where):
    return pltpu.make_async_remote_copy(
        src_ref=src,
        dst_ref=dst,
        send_sem=send_sem,
        recv_sem=recv_sem,
        device_id=where,
        device_id_type=MESH,
    )


def split(value):
    one = value.astype(BF16)
    rest = value - one.astype(F32)
    two = rest.astype(BF16)
    return [one, two, (rest - two.astype(F32)).astype(BF16)]


def floats(terms):
    return [term.astype(F32) for term in terms]


def kernel(
    cand_hbm,
    points_hbm,
    rates_hbm,
    weights_hbm,
    component_hbm,
    prior_hbm,
    panel_hbm,
    earlier_hbm,
    diag_hbm,
    coupling_hbm,
    mean_ref,
    variance_ref,
    gradient_ref,
    panel,
    earlier,
    diag,
    coupling,
    cand,
    rates,
    prior,
    component,
    pack,
    packs,
    left,
    right,
    by_selector,
    by_points,
    part,
    core_in,
    pair,
    pair_in,
    plane,
    z_in,
    both,
    both_in,
    plane_in,
    own_cross,
    sums,
    panel_sem,
    earlier_sem,
    small_sem,
    pack_send,
    pack_recv,
    core_send,
    core_recv,
    pair_send,
    pair_recv,
    z_send,
    z_recv,
    sums_send,
    sums_recv,
):
    row = lax.axis_index("row")
    col = lax.axis_index("col")
    core = lax.rem(row, 2)
    z = lax.rem(row // 2, ZS)
    x = row // (2 * ZS)

    half = lax.rem(core + x + z // 4, 2)
    place = (half * 2 + x) * ZS + z
    others = [lax.rem(z + turn, ZS) for turn in TURNS]
    firsts = (16 * x, 16 * (1 - x))
    holds = [lax.rem(half + x + other // 4, 2) for other in others]
    mates = (
        [firsts[0] + 2 * other + hold for other, hold in zip(others, holds)],
        [firsts[1] + 2 * other + 1 - hold for other, hold in zip(others, holds)],
    )
    sibling = 2 * (row // 2) + 1 - core
    across = mates[1][ZS - 1]

    def rows_of(c):
        return pl.ds(STARTS[c], SIZES[c])

    barrier = pltpu.get_barrier_semaphore()

    def greet_col(i, carry):
        pl.semaphore_signal(
            barrier, inc=1, device_id={"col": lax.rem(col + i, 8)}, device_id_type=MESH
        )
        return carry

    panel_in = [
        pltpu.make_async_copy(
            panel_hbm.at[rows_of(c)], panel.at[rows_of(c)], panel_sem.at[c]
        )
        for c in range(CHUNKS)
    ]
    deep = DEPTH // BPARTS
    earlier_in = [
        pltpu.make_async_copy(
            earlier_hbm.at[pl.ds(i * deep, deep)], earlier.at[pl.ds(i * deep, deep)], earlier_sem.at[i]
        )
        for i in range(BPARTS)
    ]
    small_in = [
        pltpu.make_async_copy(points_hbm, pack.at[pl.ds(0, DIM)], small_sem.at[0]),
        pltpu.make_async_copy(weights_hbm, pack.at[pl.ds(DIM, 1)], small_sem.at[1]),
        pltpu.make_async_copy(component_hbm, component, small_sem.at[2]),
        pltpu.make_async_copy(cand_hbm, cand, small_sem.at[3]),
        pltpu.make_async_copy(rates_hbm, rates, small_sem.at[4]),
        pltpu.make_async_copy(prior_hbm, prior, small_sem.at[5]),
        pltpu.make_async_copy(diag_hbm, diag, small_sem.at[6]),
        pltpu.make_async_copy(coupling_hbm, coupling, small_sem.at[7]),
    ]
    panel_in[0].start()
    for copy in earlier_in:
        copy.start()
    for copy in small_in[:6]:
        copy.start()
    for at in mates[0][: ZS - 1] + mates[1] + [sibling]:
        pl.semaphore_signal(barrier, inc=1, device_id={"row": at}, device_id_type=MESH)
    lax.fori_loop(1, 8, greet_col, 0)
    panel_in[0].wait()
    for copy in earlier_in[: BPARTS // 2]:
        copy.wait()
    panel_in[1].start()

    core_copies = [
        remote(
            part.at[pl.ds(pl.multiple_of((1 - half) * HALF, HALF), HALF), rows_of(c)],
            core_in.at[:, rows_of(c)],
            core_send.at[c],
            core_recv.at[c],
            row=sibling,
        )
        for c in range(CHUNKS)
    ]
    def pair_copy(c):
        if KINDS[c] == "b":
            return remote(
                both.at[1 - x, :, rows_of(c)],
                plane_in.at[:, rows_of(c)],
                pair_send.at[c],
                pair_recv.at[c],
                row=across,
            )
        return remote(
            pair.at[1 - x, :, :, rows_of(c)],
            pair_in.at[:, :, rows_of(c)],
            pair_send.at[c],
            pair_recv.at[c],
            row=across,
        )

    def z_copies(c):
        if KINDS[c] == "b":
            ref = both_in.at[:, :, :, rows_of(c)]
        else:
            ref = z_in.at[pl.ds(0, 15 if KINDS[c] == "d" else 7), :, rows_of(c)]
        return remote(ref, ref, z_send.at[c], z_recv.at[c], row=row)

    def core_sum(c):
        core_copies[c].wait_recv()
        mine = part[pl.ds(pl.multiple_of(half * HALF, HALF), HALF), rows_of(c)].astype(F32)
        total = (mine + core_in[:, rows_of(c)].astype(F32)).astype(BF16)
        pair[:, :, :, rows_of(c)] = total.reshape(2, ZS, OWN, SIZES[c])
        if KINDS[c] == "a":
            pair_copy(c).start()
        elif KINDS[c] == "b":
            for i in range(ZS - 1):
                remote(
                    pair.at[:, others[i], :, rows_of(c)],
                    both_in.at[i, :, :, rows_of(c)],
                    z_send.at[c],
                    z_recv.at[c],
                    row=mates[0][i],
                ).start()
        else:
            for i in range(ZS):
                for away in (1, 0):
                    if i < ZS - 1 or away:
                        x_at = 1 - x if away else x
                        remote(
                            pair.at[x_at, others[i], :, rows_of(c)],
                            z_in.at[i + away * (ZS - 1), :, rows_of(c)],
                            z_send.at[c],
                            z_recv.at[c],
                            row=mates[away][i],
                        ).start()

    def pair_sum(c):
        if KINDS[c] == "a":
            pair_copy(c).wait_recv()
            total = pair[x, :, :, rows_of(c)].astype(F32) + pair_in[:, :, rows_of(c)].astype(F32)
            plane[:, :, rows_of(c)] = total.astype(BF16)
            for i in range(ZS - 1):
                remote(
                    plane.at[others[i], :, rows_of(c)],
                    z_in.at[i, :, rows_of(c)],
                    z_send.at[c],
                    z_recv.at[c],
                    row=mates[0][i],
                ).start()
        elif KINDS[c] == "b":
            z_copies(c).wait_recv()
            total = pair[:, z, :, rows_of(c)].astype(F32)
            for i in range(ZS - 1):
                total += both_in[i, :, :, rows_of(c)].astype(F32)
            both[:, :, rows_of(c)] = total.astype(BF16)
            pair_copy(c).start()

    for c in range(CHUNKS):
        if c:
            panel_in[c].wait()
        if c:
            wide = CAND // PARTS
            for i in range(PARTS):
                product = jnp.dot(
                    panel[rows_of(c)], earlier[:, i * wide : (i + 1) * wide], preferred_element_type=F32
                )
                part[pl.ds(i * wide, wide), rows_of(c)] = product.astype(BF16).T
        else:
            product = jnp.zeros((SIZES[0], CAND), F32)
            for i in range(0, BPARTS, BPARTS // 2):
                if i:
                    for copy in earlier_in[BPARTS // 2 :]:
                        copy.wait()
                    for copy in panel_in[2:] + small_in[6:]:
                        copy.start()
                product += jnp.dot(
                    panel[rows_of(c), pl.ds(i * deep, deep * BPARTS // 2)],
                    earlier[pl.ds(i * deep, deep * BPARTS // 2)],
                    preferred_element_type=F32,
                )
            part[:, rows_of(c)] = product.astype(BF16).T
        if c == 0:
            for copy in small_in[:6]:
                copy.wait()
            pack[pl.ds(DIM + 1, 7)] = jnp.zeros((7, 128), F32)
            pack[pl.ds(DIM + 1, 1)] = component[...].astype(F32)
            packs[pl.ds(col, 1)] = pack[...][None]
            pl.semaphore_wait(barrier, 15 + 7 + 1)
        core_copies[c].start()
        if c == 0:

            def give_pack(i, carry):
                remote(
                    pack, packs.at[col], pack_send, pack_recv, col=lax.rem(col + i, 8)
                ).start()
                return carry

            lax.fori_loop(1, 8, give_pack, 0)
        if c:
            core_sum(c - 1)
    core_sum(CHUNKS - 1)

    for c in ORDER:
        pair_sum(c)

    packs_moved = remote(
        packs.at[pl.ds(0, 7)], packs.at[pl.ds(0, 7)], pack_send, pack_recv, col=col
    )
    packs_moved.wait_recv()
    lane = lax.broadcasted_iota(jnp.int32, (DIM, DIM), 1)
    level = lax.broadcasted_iota(jnp.int32, (DIM, DIM), 0)
    rate = jnp.sum(jnp.where(lane == level, rates[...], 0.0), axis=1, keepdims=True)
    points = jnp.concatenate([packs[j, :DIM] for j in range(8)], axis=1)
    weights = jnp.concatenate([packs[j, DIM : DIM + 1] for j in range(8)], axis=1)
    kinds = jnp.concatenate([packs[j, DIM + 1 : DIM + 2] for j in range(8)], axis=1)
    scaled = points * rate
    levels = lax.broadcasted_iota(jnp.int32, (DIM, ROWS), 0)
    selector = jnp.where(kinds == (levels + 1).astype(F32), rate, 0.0)
    offset = jnp.where(kinds == 0.0, 1.0, 0.0) - jnp.sum(selector * points, axis=0, keepdims=True)
    point_norm = -0.5 * jnp.sum(scaled * points, axis=0, keepdims=True)
    spread = cand[...]
    cand_norm = -0.5 * jnp.sum(rate * spread * spread, axis=0, keepdims=True)

    def rows_in(shape, first, second):
        at = lax.broadcasted_iota(jnp.int32, shape, 0)
        result = jnp.zeros(shape, F32)
        for i, row_value in enumerate(first + second):
            result = jnp.where(at == i, row_value, result)
        return result.astype(BF16)

    def right_side(factor, first, second):
        one, two, three = split(factor)
        return jnp.concatenate(
            [one, two, one, three, two, one, rows_in((DIM, ROWS), first, second)], axis=0
        )

    ones = [1.0, 1.0, 1.0]
    right[:, :ROWS] = right_side(scaled, floats(split(point_norm)), ones)
    right[:, ROWS:] = right_side(selector, floats(split(offset)), [0.0, 0.0, 0.0])
    one, two, three = split(spread)
    left[:, : 7 * DIM] = jnp.concatenate(
        [one, one, two, one, two, three, rows_in((DIM, CAND), ones, floats(split(cand_norm)))],
        axis=0,
    ).T
    by_selector[...] = jnp.concatenate(split(selector * weights)[:2], axis=0)
    by_points[: 2 * DIM] = jnp.concatenate(split(points * weights)[:2], axis=0)
    by_points[2 * DIM :] = rows_in((DIM, ROWS), floats(split(weights)), [])

    def assemble(some):
        both = jnp.dot(some, right[...], preferred_element_type=F32)
        near = jnp.exp(both[:, :ROWS])
        return near, near * both[:, ROWS:]

    own_cross[...] = assemble(
        left[pl.ds(pl.multiple_of(place * OWN, OWN), OWN), : 7 * DIM]
    )[1]

    def residual(c):
        if KINDS[c] == "b":
            pair_copy(c).wait_recv()
            total = both[x, :, rows_of(c)].astype(F32) + plane_in[:, rows_of(c)].astype(F32)
        else:
            z_copies(c).wait_recv()
            total = pair[x, z, :, rows_of(c)] if KINDS[c] == "d" else plane[z, :, rows_of(c)]
            total = total.astype(F32)
            for i in range(15 if KINDS[c] == "d" else 7):
                total += z_in[i, :, rows_of(c)].astype(F32)
        return (own_cross[:, rows_of(c)] - total).astype(BF16)

    def nt(a, b):
        return lax.dot_general(a, b, NT, preferred_element_type=F32)

    small_in[6].wait()
    small_in[7].wait()
    first_rhs = jnp.concatenate([residual(c) for c in range(CHUNKS) if STARTS[c] < 512], axis=1)
    block_one = nt(first_rhs, diag[0]).astype(BF16)
    coupled = nt(block_one, coupling[...])
    one = block_one.astype(F32)
    squares = jnp.sum(one * one, axis=1, keepdims=True)
    second = jnp.concatenate([residual(c) for c in range(CHUNKS) if STARTS[c] >= 512], axis=1)
    second_rhs = (second.astype(F32) - coupled).astype(BF16)
    two = nt(second_rhs, diag[1]).astype(BF16).astype(F32)
    squares += jnp.sum(two * two, axis=1, keepdims=True)
    lane = lax.broadcasted_iota(jnp.int32, (OWN, QUARTER), 1)
    number = lax.broadcasted_iota(jnp.int32, (OWN, QUARTER), 0)
    sums[pl.ds(place, 1)] = jnp.sum(
        jnp.where(lane == number + z * OWN, squares, 0.0), axis=0, keepdims=True
    )

    for i in range(ZS):
        for first in firsts[::-1]:
            for at in (1 - core, core):
                if i < ZS - 1 or first is not firsts[0] or at is not core:
                    remote(
                        sums.at[pl.ds(place, 1)],
                        sums.at[pl.ds(place, 1)],
                        sums_send,
                        sums_recv,
                        row=first + 2 * others[i] + at,
                    ).start()

    for q in range(4):
        some = pl.ds(q * QUARTER, QUARTER)
        near, cross = assemble(left[some, : 7 * DIM])
        near_one, near_two, _ = split(near)
        cross_one, cross_two, _ = split(cross)
        by_near = (nt(near_one, by_selector[...]) + nt(near_two, by_selector[...])).T
        by_cross = (nt(cross_one, by_points[...]) + nt(cross_two, by_points[...])).T
        mean = jnp.sum(by_cross[2 * DIM :], axis=0, keepdims=True)
        mean_ref[:, some] = mean
        gradient_ref[:, some] = (by_near[:DIM] + by_near[DIM:]) - rate * (
            cand[:, some] * mean - (by_cross[:DIM] + by_cross[DIM : 2 * DIM])
        )

    remote(
        sums.at[pl.ds(0, 4 * ZS - 1)], sums.at[pl.ds(0, 4 * ZS - 1)], sums_send, sums_recv, row=row
    ).wait()
    for q in range(4):
        variance_ref[:, pl.ds(q * QUARTER, QUARTER)] = prior[
            :, pl.ds(q * QUARTER, QUARTER)
        ] - jnp.sum(sums[pl.ds(q * ZS, ZS)], axis=0, keepdims=True)

    packs_moved.wait_send()
    for c in range(CHUNKS):
        core_copies[c].wait_send()
        z_copies(c).wait_send()
        if KINDS[c] != "d":
            pair_copy(c).wait_send()


def deliver(mean, variance, gradient, mean_out, variance_out, gradient_out):
    mean_out[...] = mean[...]
    variance_out[...] = variance[...]
    gradient_out[...] = gradient[...]


def shards(
    candidates,
    train_pts,
    length_rates,
    kriging_weights,
    component,
    prior_var,
    factor_panel,
    earlier_solution,
    diag_inverse,
    coupling,
):
    dma = pltpu.SemaphoreType.DMA
    shapes = (
        jax.ShapeDtypeStruct((1, CAND), F32),
        jax.ShapeDtypeStruct((1, CAND), F32),
        jax.ShapeDtypeStruct((DIM, CAND), F32),
    )
    mean, variance, gradient = pl.pallas_call(
        kernel,
        out_shape=tuple(pltpu.VMEM(shape.shape, F32) for shape in shapes),
        in_specs=[pl.BlockSpec(memory_space=pltpu.HBM)] * 10,
        out_specs=[pl.BlockSpec(memory_space=pltpu.VMEM)] * 3,
        scratch_shapes=[
            pltpu.VMEM((ROWS, DEPTH), BF16),
            pltpu.VMEM((DEPTH, CAND), BF16),
            pltpu.VMEM((2, 512, 512), BF16),
            pltpu.VMEM((512, 512), BF16),
            pltpu.VMEM((DIM, CAND), F32),
            pltpu.VMEM((1, DIM), F32),
            pltpu.VMEM((1, CAND), F32),
            pltpu.VMEM((1, 128), jnp.int32),
            pltpu.VMEM((DIM + 8, 128), F32),
            pltpu.VMEM((8, DIM + 8, 128), F32),
            pltpu.VMEM((CAND, 8 * DIM), BF16),
            pltpu.VMEM((7 * DIM, 2 * ROWS), BF16),
            pltpu.VMEM((2 * DIM, ROWS), BF16),
            pltpu.VMEM((3 * DIM, ROWS), BF16),
            pltpu.VMEM((CAND, ROWS), BF16),
            pltpu.VMEM((HALF, ROWS), BF16),
            pltpu.VMEM((2, ZS, OWN, ROWS), BF16),
            pltpu.VMEM((ZS, OWN, ROWS), BF16),
            pltpu.VMEM((ZS, OWN, ROWS), BF16),
            pltpu.VMEM((2 * ZS - 1, OWN, ROWS), BF16),
            pltpu.VMEM((2, OWN, ROWS), BF16),
            pltpu.VMEM((ZS - 1, 2, OWN, ROWS), BF16),
            pltpu.VMEM((OWN, ROWS), BF16),
            pltpu.VMEM((OWN, ROWS), F32),
            pltpu.VMEM((4 * ZS, 128), F32),
            dma((CHUNKS,)),
            dma((BPARTS,)),
            dma((8,)),
            dma,
            dma,
            dma((CHUNKS,)),
            dma((CHUNKS,)),
            dma((CHUNKS,)),
            dma((CHUNKS,)),
            dma((CHUNKS,)),
            dma((CHUNKS,)),
            dma,
            dma,
        ],
        compiler_params=pltpu.CompilerParams(
            collective_id=0, has_side_effects=True, vmem_limit_bytes=56 << 20
        ),
    )(
        candidates,
        train_pts,
        length_rates.reshape(1, DIM),
        kriging_weights.reshape(1, -1),
        component.reshape(1, -1),
        prior_var.reshape(1, CAND),
        factor_panel,
        earlier_solution,
        diag_inverse,
        coupling,
    )
    whole = pl.BlockSpec(memory_space=pltpu.VMEM)
    mean, variance, gradient = pl.pallas_call(
        deliver, out_shape=shapes, in_specs=[whole] * 3, out_specs=[whole] * 3
    )(mean, variance, gradient)
    return mean.reshape(CAND), variance.reshape(CAND), gradient


def solution(mesh):
    return jax.shard_map(
        shards,
        mesh=mesh,
        in_specs=(
            P(None, "col"),
            P(None, "col"),
            P(),
            P("col"),
            P("col"),
            P("col"),
            P(None, "row"),
            P("row", "col"),
            P(),
            P(),
        ),
        out_specs=(P("col"), P("col"), P(None, "col")),
        check_vma=False,
    )
```

```python
import jax
import jax.numpy as jnp
from jax import lax
from jax.experimental import pallas as pl
from jax.experimental.pallas import tpu as pltpu
from jax.sharding import PartitionSpec as P

MESH = pl.DeviceIdType.MESH
F32 = jnp.float32
BF16 = jnp.bfloat16
NT = (((1,), (1,)), ((), ()))

ROWS = 1024
CAND = 512
DEPTH = 3072
DIM = 32
PARTS = 1
SIZES = (256, 256, 256, 256)
KINDS = "baad"
ORDER = (1, 2, 0)
HALF = CAND // 2
QUARTER = CAND // 4
OWN = CAND // 32
ZS = 8
CHUNKS = len(SIZES)
STARTS = tuple(sum(SIZES[:c]) for c in range(CHUNKS))
TURNS = (4, 3, 5, 2, 6, 1, 7, 0)
BPARTS = 4


def remote(src, dst, send_sem, recv_sem, **where):
    return pltpu.make_async_remote_copy(
        src_ref=src,
        dst_ref=dst,
        send_sem=send_sem,
        recv_sem=recv_sem,
        device_id=where,
        device_id_type=MESH,
    )


def split(value):
    one = value.astype(BF16)
    rest = value - one.astype(F32)
    two = rest.astype(BF16)
    return [one, two, (rest - two.astype(F32)).astype(BF16)]


def floats(terms):
    return [term.astype(F32) for term in terms]


def kernel(
    cand_hbm,
    points_hbm,
    rates_hbm,
    weights_hbm,
    component_hbm,
    prior_hbm,
    panel_hbm,
    earlier_hbm,
    diag_hbm,
    coupling_hbm,
    mean_ref,
    variance_ref,
    gradient_ref,
    panel,
    earlier,
    diag,
    coupling,
    cand,
    rates,
    prior,
    component,
    pack,
    packs,
    left,
    right,
    by_selector,
    by_points,
    part,
    core_in,
    pair,
    pair_in,
    plane,
    z_in,
    both,
    both_in,
    plane_in,
    own_cross,
    sums,
    panel_sem,
    earlier_sem,
    small_sem,
    pack_send,
    pack_recv,
    core_send,
    core_recv,
    pair_send,
    pair_recv,
    z_send,
    z_recv,
    sums_send,
    sums_recv,
):
    row = lax.axis_index("row")
    col = lax.axis_index("col")
    core = lax.rem(row, 2)
    z = lax.rem(row // 2, ZS)
    x = row // (2 * ZS)

    half = lax.rem(core + x + z // 4, 2)
    place = (half * 2 + x) * ZS + z
    others = [lax.rem(z + turn, ZS) for turn in TURNS]
    firsts = (16 * x, 16 * (1 - x))
    holds = [lax.rem(half + x + other // 4, 2) for other in others]
    mates = (
        [firsts[0] + 2 * other + hold for other, hold in zip(others, holds)],
        [firsts[1] + 2 * other + 1 - hold for other, hold in zip(others, holds)],
    )
    sibling = 2 * (row // 2) + 1 - core
    across = mates[1][ZS - 1]

    def rows_of(c):
        return pl.ds(STARTS[c], SIZES[c])

    barrier = pltpu.get_barrier_semaphore()

    def greet_col(i, carry):
        pl.semaphore_signal(
            barrier, inc=1, device_id={"col": lax.rem(col + i, 8)}, device_id_type=MESH
        )
        return carry

    panel_in = [
        pltpu.make_async_copy(
            panel_hbm.at[rows_of(c)], panel.at[rows_of(c)], panel_sem.at[c]
        )
        for c in range(CHUNKS)
    ]
    deep = DEPTH // BPARTS
    earlier_in = [
        pltpu.make_async_copy(
            earlier_hbm.at[pl.ds(i * deep, deep)], earlier.at[pl.ds(i * deep, deep)], earlier_sem.at[i]
        )
        for i in range(BPARTS)
    ]
    small_in = [
        pltpu.make_async_copy(points_hbm, pack.at[pl.ds(0, DIM)], small_sem.at[0]),
        pltpu.make_async_copy(weights_hbm, pack.at[pl.ds(DIM, 1)], small_sem.at[1]),
        pltpu.make_async_copy(component_hbm, component, small_sem.at[2]),
        pltpu.make_async_copy(cand_hbm, cand, small_sem.at[3]),
        pltpu.make_async_copy(rates_hbm, rates, small_sem.at[4]),
        pltpu.make_async_copy(prior_hbm, prior, small_sem.at[5]),
        pltpu.make_async_copy(diag_hbm, diag, small_sem.at[6]),
        pltpu.make_async_copy(coupling_hbm, coupling, small_sem.at[7]),
    ]
    panel_in[0].start()
    for copy in earlier_in:
        copy.start()
    for copy in small_in[:6]:
        copy.start()
    for at in mates[0][: ZS - 1] + mates[1] + [sibling]:
        pl.semaphore_signal(barrier, inc=1, device_id={"row": at}, device_id_type=MESH)
    lax.fori_loop(1, 8, greet_col, 0)
    panel_in[0].wait()
    for copy in earlier_in[: BPARTS // 2]:
        copy.wait()
    panel_in[1].start()

    core_copies = [
        remote(
            part.at[pl.ds(pl.multiple_of((1 - half) * HALF, HALF), HALF), rows_of(c)],
            core_in.at[:, rows_of(c)],
            core_send.at[c],
            core_recv.at[c],
            row=sibling,
        )
        for c in range(CHUNKS)
    ]
    def pair_copy(c):
        if KINDS[c] == "b":
            return remote(
                both.at[1 - x, :, rows_of(c)],
                plane_in.at[:, rows_of(c)],
                pair_send.at[c],
                pair_recv.at[c],
                row=across,
            )
        return remote(
            pair.at[1 - x, :, :, rows_of(c)],
            pair_in.at[:, :, rows_of(c)],
            pair_send.at[c],
            pair_recv.at[c],
            row=across,
        )

    def z_copies(c):
        if KINDS[c] == "b":
            ref = both_in.at[:, :, :, rows_of(c)]
        else:
            ref = z_in.at[pl.ds(0, 15 if KINDS[c] == "d" else 7), :, rows_of(c)]
        return remote(ref, ref, z_send.at[c], z_recv.at[c], row=row)

    def core_sum(c):
        core_copies[c].wait_recv()
        mine = part[pl.ds(pl.multiple_of(half * HALF, HALF), HALF), rows_of(c)].astype(F32)
        total = (mine + core_in[:, rows_of(c)].astype(F32)).astype(BF16)
        pair[:, :, :, rows_of(c)] = total.reshape(2, ZS, OWN, SIZES[c])
        if KINDS[c] == "a":
            pair_copy(c).start()
        elif KINDS[c] == "b":
            for i in range(ZS - 1):
                remote(
                    pair.at[:, others[i], :, rows_of(c)],
                    both_in.at[i, :, :, rows_of(c)],
                    z_send.at[c],
                    z_recv.at[c],
                    row=mates[0][i],
                ).start()
        else:
            for i in range(ZS):
                for away in (1, 0):
                    if i < ZS - 1 or away:
                        x_at = 1 - x if away else x
                        remote(
                            pair.at[x_at, others[i], :, rows_of(c)],
                            z_in.at[i + away * (ZS - 1), :, rows_of(c)],
                            z_send.at[c],
                            z_recv.at[c],
                            row=mates[away][i],
                        ).start()

    def pair_sum(c):
        if KINDS[c] == "a":
            pair_copy(c).wait_recv()
            total = pair[x, :, :, rows_of(c)].astype(F32) + pair_in[:, :, rows_of(c)].astype(F32)
            plane[:, :, rows_of(c)] = total.astype(BF16)
            for i in range(ZS - 1):
                remote(
                    plane.at[others[i], :, rows_of(c)],
                    z_in.at[i, :, rows_of(c)],
                    z_send.at[c],
                    z_recv.at[c],
                    row=mates[0][i],
                ).start()
        elif KINDS[c] == "b":
            z_copies(c).wait_recv()
            total = pair[:, z, :, rows_of(c)].astype(F32)
            for i in range(ZS - 1):
                total += both_in[i, :, :, rows_of(c)].astype(F32)
            both[:, :, rows_of(c)] = total.astype(BF16)
            pair_copy(c).start()

    for c in range(CHUNKS):
        if c:
            panel_in[c].wait()
        if c:
            wide = CAND // PARTS
            for i in range(PARTS):
                product = jnp.dot(
                    panel[rows_of(c)], earlier[:, i * wide : (i + 1) * wide], preferred_element_type=F32
                )
                part[pl.ds(i * wide, wide), rows_of(c)] = product.astype(BF16).T
        else:
            product = jnp.zeros((SIZES[0], CAND), F32)
            for i in range(0, BPARTS, BPARTS // 2):
                if i:
                    for copy in earlier_in[BPARTS // 2 :]:
                        copy.wait()
                    for copy in panel_in[2:] + small_in[6:]:
                        copy.start()
                product += jnp.dot(
                    panel[rows_of(c), pl.ds(i * deep, deep * BPARTS // 2)],
                    earlier[pl.ds(i * deep, deep * BPARTS // 2)],
                    preferred_element_type=F32,
                )
            part[:, rows_of(c)] = product.astype(BF16).T
        if c == 0:
            for copy in small_in[:6]:
                copy.wait()
            pack[pl.ds(DIM + 1, 7)] = jnp.zeros((7, 128), F32)
            pack[pl.ds(DIM + 1, 1)] = component[...].astype(F32)
            packs[pl.ds(col, 1)] = pack[...][None]
            pl.semaphore_wait(barrier, 15 + 7 + 1)
        core_copies[c].start()
        if c == 0:

            def give_pack(i, carry):
                remote(
                    pack, packs.at[col], pack_send, pack_recv, col=lax.rem(col + i, 8)
                ).start()
                return carry

            lax.fori_loop(1, 8, give_pack, 0)
        if c:
            core_sum(c - 1)
    core_sum(CHUNKS - 1)

    for c in ORDER:
        pair_sum(c)

    packs_moved = remote(
        packs.at[pl.ds(0, 7)], packs.at[pl.ds(0, 7)], pack_send, pack_recv, col=col
    )
    packs_moved.wait_recv()
    lane = lax.broadcasted_iota(jnp.int32, (DIM, DIM), 1)
    level = lax.broadcasted_iota(jnp.int32, (DIM, DIM), 0)
    rate = jnp.sum(jnp.where(lane == level, rates[...], 0.0), axis=1, keepdims=True)
    points = jnp.concatenate([packs[j, :DIM] for j in range(8)], axis=1)
    weights = jnp.concatenate([packs[j, DIM : DIM + 1] for j in range(8)], axis=1)
    kinds = jnp.concatenate([packs[j, DIM + 1 : DIM + 2] for j in range(8)], axis=1)
    scaled = points * rate
    levels = lax.broadcasted_iota(jnp.int32, (DIM, ROWS), 0)
    selector = jnp.where(kinds == (levels + 1).astype(F32), rate, 0.0)
    offset = jnp.where(kinds == 0.0, 1.0, 0.0) - jnp.sum(selector * points, axis=0, keepdims=True)
    point_norm = -0.5 * jnp.sum(scaled * points, axis=0, keepdims=True)
    spread = cand[...]
    cand_norm = -0.5 * jnp.sum(rate * spread * spread, axis=0, keepdims=True)

    def rows_in(shape, first, second):
        at = lax.broadcasted_iota(jnp.int32, shape, 0)
        result = jnp.zeros(shape, F32)
        for i, row_value in enumerate(first + second):
            result = jnp.where(at == i, row_value, result)
        return result.astype(BF16)

    def right_side(factor, first, second):
        one, two, three = split(factor)
        return jnp.concatenate(
            [one, two, one, three, two, one, rows_in((DIM, ROWS), first, second)], axis=0
        )

    ones = [1.0, 1.0, 1.0]
    right[:, :ROWS] = right_side(scaled, floats(split(point_norm)), ones)
    right[:, ROWS:] = right_side(selector, floats(split(offset)), [0.0, 0.0, 0.0])
    one, two, three = split(spread)
    left[:, : 7 * DIM] = jnp.concatenate(
        [one, one, two, one, two, three, rows_in((DIM, CAND), ones, floats(split(cand_norm)))],
        axis=0,
    ).T
    by_selector[...] = jnp.concatenate(split(selector * weights)[:2], axis=0)
    by_points[: 2 * DIM] = jnp.concatenate(split(points * weights)[:2], axis=0)
    by_points[2 * DIM :] = rows_in((DIM, ROWS), floats(split(weights)), [])

    def assemble(some):
        both = jnp.dot(some, right[...], preferred_element_type=F32)
        near = jnp.exp(both[:, :ROWS])
        return near, near * both[:, ROWS:]

    own_cross[...] = assemble(
        left[pl.ds(pl.multiple_of(place * OWN, OWN), OWN), : 7 * DIM]
    )[1]

    def residual(c):
        if KINDS[c] == "b":
            pair_copy(c).wait_recv()
            total = both[x, :, rows_of(c)].astype(F32) + plane_in[:, rows_of(c)].astype(F32)
        else:
            z_copies(c).wait_recv()
            total = pair[x, z, :, rows_of(c)] if KINDS[c] == "d" else plane[z, :, rows_of(c)]
            total = total.astype(F32)
            for i in range(15 if KINDS[c] == "d" else 7):
                total += z_in[i, :, rows_of(c)].astype(F32)
        return (own_cross[:, rows_of(c)] - total).astype(BF16)

    def nt(a, b):
        return lax.dot_general(a, b, NT, preferred_element_type=F32)

    small_in[6].wait()
    small_in[7].wait()
    first_rhs = jnp.concatenate([residual(c) for c in range(CHUNKS) if STARTS[c] < 512], axis=1)
    block_one = nt(first_rhs, diag[0]).astype(BF16)
    coupled = nt(block_one, coupling[...])
    one = block_one.astype(F32)
    squares = jnp.sum(one * one, axis=1, keepdims=True)
    second = jnp.concatenate([residual(c) for c in range(CHUNKS) if STARTS[c] >= 512], axis=1)
    second_rhs = (second.astype(F32) - coupled).astype(BF16)
    two = nt(second_rhs, diag[1]).astype(BF16).astype(F32)
    squares += jnp.sum(two * two, axis=1, keepdims=True)
    lane = lax.broadcasted_iota(jnp.int32, (OWN, QUARTER), 1)
    number = lax.broadcasted_iota(jnp.int32, (OWN, QUARTER), 0)
    sums[pl.ds(place, 1)] = jnp.sum(
        jnp.where(lane == number + z * OWN, squares, 0.0), axis=0, keepdims=True
    )

    for i in range(ZS):
        for first in firsts[::-1]:
            for at in (1 - core, core):
                if i < ZS - 1 or first is not firsts[0] or at is not core:
                    remote(
                        sums.at[pl.ds(place, 1)],
                        sums.at[pl.ds(place, 1)],
                        sums_send,
                        sums_recv,
                        row=first + 2 * others[i] + at,
                    ).start()

    for q in range(4):
        some = pl.ds(q * QUARTER, QUARTER)
        near, cross = assemble(left[some, : 7 * DIM])
        near_one, near_two, _ = split(near)
        cross_one, cross_two, _ = split(cross)
        by_near = (nt(near_one, by_selector[...]) + nt(near_two, by_selector[...])).T
        by_cross = (nt(cross_one, by_points[...]) + nt(cross_two, by_points[...])).T
        mean = jnp.sum(by_cross[2 * DIM :], axis=0, keepdims=True)
        mean_ref[:, some] = mean
        gradient_ref[:, some] = (by_near[:DIM] + by_near[DIM:]) - rate * (
            cand[:, some] * mean - (by_cross[:DIM] + by_cross[DIM : 2 * DIM])
        )

    packs_moved.wait_send()
    for c in range(CHUNKS):
        core_copies[c].wait_send()
        z_copies(c).wait_send()
        if KINDS[c] != "d":
            pair_copy(c).wait_send()

    remote(
        sums.at[pl.ds(0, 4 * ZS - 1)], sums.at[pl.ds(0, 4 * ZS - 1)], sums_send, sums_recv, row=row
    ).wait()
    for q in range(4):
        variance_ref[:, pl.ds(q * QUARTER, QUARTER)] = prior[
            :, pl.ds(q * QUARTER, QUARTER)
        ] - jnp.sum(sums[pl.ds(q * ZS, ZS)], axis=0, keepdims=True)


def deliver(mean, variance, gradient, mean_out, variance_out, gradient_out):
    mean_out[...] = mean[...]
    variance_out[...] = variance[...]
    gradient_out[...] = gradient[...]


def shards(
    candidates,
    train_pts,
    length_rates,
    kriging_weights,
    component,
    prior_var,
    factor_panel,
    earlier_solution,
    diag_inverse,
    coupling,
):
    dma = pltpu.SemaphoreType.DMA
    shapes = (
        jax.ShapeDtypeStruct((1, CAND), F32),
        jax.ShapeDtypeStruct((1, CAND), F32),
        jax.ShapeDtypeStruct((DIM, CAND), F32),
    )
    mean, variance, gradient = pl.pallas_call(
        kernel,
        out_shape=tuple(pltpu.VMEM(shape.shape, F32) for shape in shapes),
        in_specs=[pl.BlockSpec(memory_space=pltpu.HBM)] * 10,
        out_specs=[pl.BlockSpec(memory_space=pltpu.VMEM)] * 3,
        scratch_shapes=[
            pltpu.VMEM((ROWS, DEPTH), BF16),
            pltpu.VMEM((DEPTH, CAND), BF16),
            pltpu.VMEM((2, 512, 512), BF16),
            pltpu.VMEM((512, 512), BF16),
            pltpu.VMEM((DIM, CAND), F32),
            pltpu.VMEM((1, DIM), F32),
            pltpu.VMEM((1, CAND), F32),
            pltpu.VMEM((1, 128), jnp.int32),
            pltpu.VMEM((DIM + 8, 128), F32),
            pltpu.VMEM((8, DIM + 8, 128), F32),
            pltpu.VMEM((CAND, 8 * DIM), BF16),
            pltpu.VMEM((7 * DIM, 2 * ROWS), BF16),
            pltpu.VMEM((2 * DIM, ROWS), BF16),
            pltpu.VMEM((3 * DIM, ROWS), BF16),
            pltpu.VMEM((CAND, ROWS), BF16),
            pltpu.VMEM((HALF, ROWS), BF16),
            pltpu.VMEM((2, ZS, OWN, ROWS), BF16),
            pltpu.VMEM((ZS, OWN, ROWS), BF16),
            pltpu.VMEM((ZS, OWN, ROWS), BF16),
            pltpu.VMEM((2 * ZS - 1, OWN, ROWS), BF16),
            pltpu.VMEM((2, OWN, ROWS), BF16),
            pltpu.VMEM((ZS - 1, 2, OWN, ROWS), BF16),
            pltpu.VMEM((OWN, ROWS), BF16),
            pltpu.VMEM((OWN, ROWS), F32),
            pltpu.VMEM((4 * ZS, 128), F32),
            dma((CHUNKS,)),
            dma((BPARTS,)),
            dma((8,)),
            dma,
            dma,
            dma((CHUNKS,)),
            dma((CHUNKS,)),
            dma((CHUNKS,)),
            dma((CHUNKS,)),
            dma((CHUNKS,)),
            dma((CHUNKS,)),
            dma,
            dma,
        ],
        compiler_params=pltpu.CompilerParams(
            collective_id=0, has_side_effects=True, vmem_limit_bytes=56 << 20
        ),
    )(
        candidates,
        train_pts,
        length_rates.reshape(1, DIM),
        kriging_weights.reshape(1, -1),
        component.reshape(1, -1),
        prior_var.reshape(1, CAND),
        factor_panel,
        earlier_solution,
        diag_inverse,
        coupling,
    )
    mean, variance, gradient = [
        pltpu.with_memory_space_constraint(value, pltpu.VMEM) for value in (mean, variance, gradient)
    ]
    whole = pl.BlockSpec(memory_space=pltpu.VMEM)
    mean, variance, gradient = pl.pallas_call(
        deliver, out_shape=shapes, in_specs=[whole] * 3, out_specs=[whole] * 3
    )(mean, variance, gradient)
    return mean.reshape(CAND), variance.reshape(CAND), gradient


def solution(mesh):
    return jax.shard_map(
        shards,
        mesh=mesh,
        in_specs=(
            P(None, "col"),
            P(None, "col"),
            P(),
            P("col"),
            P("col"),
            P("col"),
            P(None, "row"),
            P("row", "col"),
            P(),
            P(),
        ),
        out_specs=(P("col"), P("col"), P(None, "col")),
        check_vma=False,
    )
```

```python
import jax
import jax.numpy as jnp
from jax import lax
from jax.experimental import pallas as pl
from jax.experimental.pallas import tpu as pltpu
from jax.sharding import PartitionSpec as P

MESH = pl.DeviceIdType.MESH
F32 = jnp.float32
BF16 = jnp.bfloat16
NT = (((1,), (1,)), ((), ()))

ROWS = 1024
CAND = 512
DEPTH = 3072
DIM = 32
PARTS = 1
MEET = 1
SUMS = ((), (), (0, 1), (2,), (3,))
SIZES = (256, 256, 256, 256)
KINDS = "baad"
ORDER = (1, 2, 0)
HALF = CAND // 2
QUARTER = CAND // 4
OWN = CAND // 32
ZS = 8
CHUNKS = len(SIZES)
STARTS = tuple(sum(SIZES[:c]) for c in range(CHUNKS))
TURNS = (4, 3, 5, 2, 6, 1, 7, 0)
BPARTS = 4


def remote(src, dst, send_sem, recv_sem, **where):
    return pltpu.make_async_remote_copy(
        src_ref=src,
        dst_ref=dst,
        send_sem=send_sem,
        recv_sem=recv_sem,
        device_id=where,
        device_id_type=MESH,
    )


def split(value):
    one = value.astype(BF16)
    rest = value - one.astype(F32)
    two = rest.astype(BF16)
    return [one, two, (rest - two.astype(F32)).astype(BF16)]


def floats(terms):
    return [term.astype(F32) for term in terms]


def kernel(
    cand_hbm,
    points_hbm,
    rates_hbm,
    weights_hbm,
    component_hbm,
    prior_hbm,
    panel_hbm,
    earlier_hbm,
    diag_hbm,
    coupling_hbm,
    mean_ref,
    variance_ref,
    gradient_ref,
    panel,
    earlier,
    diag,
    coupling,
    cand,
    rates,
    prior,
    component,
    pack,
    packs,
    left,
    right,
    by_selector,
    by_points,
    part,
    core_in,
    pair,
    pair_in,
    plane,
    z_in,
    both,
    both_in,
    plane_in,
    own_cross,
    sums,
    panel_sem,
    earlier_sem,
    small_sem,
    pack_send,
    pack_recv,
    core_send,
    core_recv,
    pair_send,
    pair_recv,
    z_send,
    z_recv,
    sums_send,
    sums_recv,
):
    row = lax.axis_index("row")
    col = lax.axis_index("col")
    core = lax.rem(row, 2)
    z = lax.rem(row // 2, ZS)
    x = row // (2 * ZS)

    half = lax.rem(core + x + z // 4, 2)
    place = (half * 2 + x) * ZS + z
    others = [lax.rem(z + turn, ZS) for turn in TURNS]
    firsts = (16 * x, 16 * (1 - x))
    holds = [lax.rem(half + x + other // 4, 2) for other in others]
    mates = (
        [firsts[0] + 2 * other + hold for other, hold in zip(others, holds)],
        [firsts[1] + 2 * other + 1 - hold for other, hold in zip(others, holds)],
    )
    sibling = 2 * (row // 2) + 1 - core
    y = lax.rem(col, 4)
    beside = firsts[1] + 2 * z + core
    columns = [{"row": beside, "col": 4 - (col - y) + lax.rem(y + turn, 4)} for turn in (2, 1, 3, 0)]
    columns += [{"row": row, "col": col - y + lax.rem(y + turn, 4)} for turn in (2, 1, 3)]
    across = mates[1][ZS - 1]

    def rows_of(c):
        return pl.ds(STARTS[c], SIZES[c])

    barrier = pltpu.get_barrier_semaphore()

    panel_in = [
        pltpu.make_async_copy(
            panel_hbm.at[rows_of(c)], panel.at[rows_of(c)], panel_sem.at[c]
        )
        for c in range(CHUNKS)
    ]
    deep = DEPTH // BPARTS
    earlier_in = [
        pltpu.make_async_copy(
            earlier_hbm.at[pl.ds(i * deep, deep)], earlier.at[pl.ds(i * deep, deep)], earlier_sem.at[i]
        )
        for i in range(BPARTS)
    ]
    small_in = [
        pltpu.make_async_copy(points_hbm, pack.at[pl.ds(0, DIM)], small_sem.at[0]),
        pltpu.make_async_copy(weights_hbm, pack.at[pl.ds(DIM, 1)], small_sem.at[1]),
        pltpu.make_async_copy(component_hbm, component, small_sem.at[2]),
        pltpu.make_async_copy(cand_hbm, cand, small_sem.at[3]),
        pltpu.make_async_copy(rates_hbm, rates, small_sem.at[4]),
        pltpu.make_async_copy(prior_hbm, prior, small_sem.at[5]),
        pltpu.make_async_copy(diag_hbm, diag, small_sem.at[6]),
        pltpu.make_async_copy(coupling_hbm, coupling, small_sem.at[7]),
    ]
    def greet():
        for device in columns:
            pl.semaphore_signal(barrier, inc=1, device_id=device, device_id_type=MESH)
        for at in mates[1][:2] + mates[0][: ZS - 1] + mates[1][2:] + [sibling]:
            pl.semaphore_signal(barrier, inc=1, device_id={"row": at}, device_id_type=MESH)

    panel_in[0].start()
    for copy in earlier_in[: BPARTS // 2]:
        copy.start()
    greet()
    for copy in earlier_in[BPARTS // 2 :]:
        copy.start()
    for copy in small_in[:6]:
        copy.start()
    panel_in[0].wait()
    for copy in earlier_in[: BPARTS // 2]:
        copy.wait()
    panel_in[1].start()

    core_copies = [
        remote(
            part.at[pl.ds(pl.multiple_of((1 - half) * HALF, HALF), HALF), rows_of(c)],
            core_in.at[:, rows_of(c)],
            core_send.at[c],
            core_recv.at[c],
            row=sibling,
        )
        for c in range(CHUNKS)
    ]
    def pair_copy(c):
        if KINDS[c] == "b":
            return remote(
                both.at[1 - x, :, rows_of(c)],
                plane_in.at[:, rows_of(c)],
                pair_send.at[c],
                pair_recv.at[c],
                row=across,
            )
        return remote(
            pair.at[1 - x, :, :, rows_of(c)],
            pair_in.at[:, :, rows_of(c)],
            pair_send.at[c],
            pair_recv.at[c],
            row=across,
        )

    def z_copies(c):
        if KINDS[c] == "b":
            ref = both_in.at[:, :, :, rows_of(c)]
        else:
            ref = z_in.at[pl.ds(0, 15 if KINDS[c] == "d" else 7), :, rows_of(c)]
        return remote(ref, ref, z_send.at[c], z_recv.at[c], row=row)

    def core_sum(c):
        core_copies[c].wait_recv()
        mine = part[pl.ds(pl.multiple_of(half * HALF, HALF), HALF), rows_of(c)].astype(F32)
        total = (mine + core_in[:, rows_of(c)].astype(F32)).astype(BF16)
        pair[:, :, :, rows_of(c)] = total.reshape(2, ZS, OWN, SIZES[c])
        if KINDS[c] == "a":
            pair_copy(c).start()
        elif KINDS[c] == "b":
            for i in range(ZS - 1):
                remote(
                    pair.at[:, others[i], :, rows_of(c)],
                    both_in.at[i, :, :, rows_of(c)],
                    z_send.at[c],
                    z_recv.at[c],
                    row=mates[0][i],
                ).start()
        else:
            for i in range(ZS):
                for away in (1, 0):
                    if i < ZS - 1 or away:
                        x_at = 1 - x if away else x
                        remote(
                            pair.at[x_at, others[i], :, rows_of(c)],
                            z_in.at[i + away * (ZS - 1), :, rows_of(c)],
                            z_send.at[c],
                            z_recv.at[c],
                            row=mates[away][i],
                        ).start()

    def pair_sum(c):
        if KINDS[c] == "a":
            pair_copy(c).wait_recv()
            total = pair[x, :, :, rows_of(c)].astype(F32) + pair_in[:, :, rows_of(c)].astype(F32)
            plane[:, :, rows_of(c)] = total.astype(BF16)
            for i in range(ZS - 1):
                remote(
                    plane.at[others[i], :, rows_of(c)],
                    z_in.at[i, :, rows_of(c)],
                    z_send.at[c],
                    z_recv.at[c],
                    row=mates[0][i],
                ).start()
        elif KINDS[c] == "b":
            z_copies(c).wait_recv()
            total = pair[:, z, :, rows_of(c)].astype(F32)
            for i in range(ZS - 1):
                total += both_in[i, :, :, rows_of(c)].astype(F32)
            both[:, :, rows_of(c)] = total.astype(BF16)
            pair_copy(c).start()

    for c in range(CHUNKS):
        if c:
            panel_in[c].wait()
        if c:
            wide = CAND // PARTS
            for i in range(PARTS):
                product = jnp.dot(
                    panel[rows_of(c)], earlier[:, i * wide : (i + 1) * wide], preferred_element_type=F32
                )
                part[pl.ds(i * wide, wide), rows_of(c)] = product.astype(BF16).T
        else:
            product = jnp.zeros((SIZES[0], CAND), F32)
            for i in range(0, BPARTS, BPARTS // 2):
                if i:
                    for copy in earlier_in[BPARTS // 2 :]:
                        copy.wait()
                    for copy in panel_in[2:] + small_in[6:]:
                        copy.start()
                product += jnp.dot(
                    panel[rows_of(c), pl.ds(i * deep, deep * BPARTS // 2)],
                    earlier[pl.ds(i * deep, deep * BPARTS // 2)],
                    preferred_element_type=F32,
                )
            part[:, rows_of(c)] = product.astype(BF16).T
        if c == 0:
            for copy in small_in[:6]:
                copy.wait()
            pack[pl.ds(DIM + 1, 7)] = jnp.zeros((7, 128), F32)
            pack[pl.ds(DIM + 1, 1)] = component[...].astype(F32)
            packs[pl.ds(col, 1)] = pack[...][None]
        if c == MEET:
            pl.semaphore_wait(barrier, 15 + 7 + 1)
            for ready in range(MEET):
                core_copies[ready].start()
        if c >= MEET:
            core_copies[c].start()
        if c == MEET:
            for device in columns:
                remote(pack, packs.at[col], pack_send, pack_recv, **device).start()
        for ready in SUMS[c]:
            core_sum(ready)
    for ready in SUMS[CHUNKS]:
        core_sum(ready)

    for c in ORDER:
        pair_sum(c)

    packs_moved = remote(
        packs.at[pl.ds(0, 7)], packs.at[pl.ds(0, 7)], pack_send, pack_recv, col=col
    )
    packs_moved.wait_recv()
    lane = lax.broadcasted_iota(jnp.int32, (DIM, DIM), 1)
    level = lax.broadcasted_iota(jnp.int32, (DIM, DIM), 0)
    rate = jnp.sum(jnp.where(lane == level, rates[...], 0.0), axis=1, keepdims=True)
    points = jnp.concatenate([packs[j, :DIM] for j in range(8)], axis=1)
    weights = jnp.concatenate([packs[j, DIM : DIM + 1] for j in range(8)], axis=1)
    kinds = jnp.concatenate([packs[j, DIM + 1 : DIM + 2] for j in range(8)], axis=1)
    scaled = points * rate
    levels = lax.broadcasted_iota(jnp.int32, (DIM, ROWS), 0)
    selector = jnp.where(kinds == (levels + 1).astype(F32), rate, 0.0)
    offset = jnp.where(kinds == 0.0, 1.0, 0.0) - jnp.sum(selector * points, axis=0, keepdims=True)
    point_norm = -0.5 * jnp.sum(scaled * points, axis=0, keepdims=True)
    spread = cand[...]
    cand_norm = -0.5 * jnp.sum(rate * spread * spread, axis=0, keepdims=True)

    def rows_in(shape, first, second):
        at = lax.broadcasted_iota(jnp.int32, shape, 0)
        result = jnp.zeros(shape, F32)
        for i, row_value in enumerate(first + second):
            result = jnp.where(at == i, row_value, result)
        return result.astype(BF16)

    def right_side(factor, first, second):
        one, two, three = split(factor)
        return jnp.concatenate(
            [one, two, one, three, two, one, rows_in((DIM, ROWS), first, second)], axis=0
        )

    ones = [1.0, 1.0, 1.0]
    right[:, :ROWS] = right_side(scaled, floats(split(point_norm)), ones)
    right[:, ROWS:] = right_side(selector, floats(split(offset)), [0.0, 0.0, 0.0])
    one, two, three = split(spread)
    left[:, : 7 * DIM] = jnp.concatenate(
        [one, one, two, one, two, three, rows_in((DIM, CAND), ones, floats(split(cand_norm)))],
        axis=0,
    ).T
    by_selector[...] = jnp.concatenate(split(selector * weights)[:2], axis=0)
    by_points[: 2 * DIM] = jnp.concatenate(split(points * weights)[:2], axis=0)
    by_points[2 * DIM :] = rows_in((DIM, ROWS), floats(split(weights)), [])

    def assemble(some):
        both = jnp.dot(some, right[...], preferred_element_type=F32)
        near = jnp.exp(both[:, :ROWS])
        return near, near * both[:, ROWS:]

    own_cross[...] = assemble(
        left[pl.ds(pl.multiple_of(place * OWN, OWN), OWN), : 7 * DIM]
    )[1]

    def residual(c):
        if KINDS[c] == "b":
            pair_copy(c).wait_recv()
            total = both[x, :, rows_of(c)].astype(F32) + plane_in[:, rows_of(c)].astype(F32)
        else:
            z_copies(c).wait_recv()
            total = pair[x, z, :, rows_of(c)] if KINDS[c] == "d" else plane[z, :, rows_of(c)]
            total = total.astype(F32)
            for i in range(15 if KINDS[c] == "d" else 7):
                total += z_in[i, :, rows_of(c)].astype(F32)
        return (own_cross[:, rows_of(c)] - total).astype(BF16)

    def nt(a, b):
        return lax.dot_general(a, b, NT, preferred_element_type=F32)

    small_in[6].wait()
    small_in[7].wait()
    first_rhs = jnp.concatenate([residual(c) for c in range(CHUNKS) if STARTS[c] < 512], axis=1)
    block_one = nt(first_rhs, diag[0]).astype(BF16)
    coupled = nt(block_one, coupling[...])
    one = block_one.astype(F32)
    squares = jnp.sum(one * one, axis=1, keepdims=True)
    second = jnp.concatenate([residual(c) for c in range(CHUNKS) if STARTS[c] >= 512], axis=1)
    second_rhs = (second.astype(F32) - coupled).astype(BF16)
    two = nt(second_rhs, diag[1]).astype(BF16).astype(F32)
    squares += jnp.sum(two * two, axis=1, keepdims=True)
    lane = lax.broadcasted_iota(jnp.int32, (OWN, QUARTER), 1)
    number = lax.broadcasted_iota(jnp.int32, (OWN, QUARTER), 0)
    sums[pl.ds(place, 1)] = jnp.sum(
        jnp.where(lane == number + z * OWN, squares, 0.0), axis=0, keepdims=True
    )

    for i in range(ZS):
        for first in firsts[::-1]:
            for at in (1 - core, core):
                if i < ZS - 1 or first is not firsts[0] or at is not core:
                    remote(
                        sums.at[pl.ds(place, 1)],
                        sums.at[pl.ds(place, 1)],
                        sums_send,
                        sums_recv,
                        row=first + 2 * others[i] + at,
                    ).start()

    for q in range(4):
        some = pl.ds(q * QUARTER, QUARTER)
        near, cross = assemble(left[some, : 7 * DIM])
        near_one, near_two, _ = split(near)
        cross_one, cross_two, _ = split(cross)
        by_near = (nt(near_one, by_selector[...]) + nt(near_two, by_selector[...])).T
        by_cross = (nt(cross_one, by_points[...]) + nt(cross_two, by_points[...])).T
        mean = jnp.sum(by_cross[2 * DIM :], axis=0, keepdims=True)
        mean_ref[:, some] = mean
        gradient_ref[:, some] = (by_near[:DIM] + by_near[DIM:]) - rate * (
            cand[:, some] * mean - (by_cross[:DIM] + by_cross[DIM : 2 * DIM])
        )

    packs_moved.wait_send()
    for c in range(CHUNKS):
        core_copies[c].wait_send()
        z_copies(c).wait_send()
        if KINDS[c] != "d":
            pair_copy(c).wait_send()

    remote(
        sums.at[pl.ds(0, 4 * ZS - 1)], sums.at[pl.ds(0, 4 * ZS - 1)], sums_send, sums_recv, row=row
    ).wait()
    for q in range(4):
        variance_ref[:, pl.ds(q * QUARTER, QUARTER)] = prior[
            :, pl.ds(q * QUARTER, QUARTER)
        ] - jnp.sum(sums[pl.ds(q * ZS, ZS)], axis=0, keepdims=True)


def deliver(mean, variance, gradient, mean_out, variance_out, gradient_out):
    mean_out[...] = mean[...]
    variance_out[...] = variance[...]
    gradient_out[...] = gradient[...]


def shards(
    candidates,
    train_pts,
    length_rates,
    kriging_weights,
    component,
    prior_var,
    factor_panel,
    earlier_solution,
    diag_inverse,
    coupling,
):
    dma = pltpu.SemaphoreType.DMA
    shapes = (
        jax.ShapeDtypeStruct((1, CAND), F32),
        jax.ShapeDtypeStruct((1, CAND), F32),
        jax.ShapeDtypeStruct((DIM, CAND), F32),
    )
    mean, variance, gradient = pl.pallas_call(
        kernel,
        out_shape=tuple(pltpu.VMEM(shape.shape, F32) for shape in shapes),
        in_specs=[pl.BlockSpec(memory_space=pltpu.HBM)] * 10,
        out_specs=[pl.BlockSpec(memory_space=pltpu.VMEM)] * 3,
        scratch_shapes=[
            pltpu.VMEM((ROWS, DEPTH), BF16),
            pltpu.VMEM((DEPTH, CAND), BF16),
            pltpu.VMEM((2, 512, 512), BF16),
            pltpu.VMEM((512, 512), BF16),
            pltpu.VMEM((DIM, CAND), F32),
            pltpu.VMEM((1, DIM), F32),
            pltpu.VMEM((1, CAND), F32),
            pltpu.VMEM((1, 128), jnp.int32),
            pltpu.VMEM((DIM + 8, 128), F32),
            pltpu.VMEM((8, DIM + 8, 128), F32),
            pltpu.VMEM((CAND, 8 * DIM), BF16),
            pltpu.VMEM((7 * DIM, 2 * ROWS), BF16),
            pltpu.VMEM((2 * DIM, ROWS), BF16),
            pltpu.VMEM((3 * DIM, ROWS), BF16),
            pltpu.VMEM((CAND, ROWS), BF16),
            pltpu.VMEM((HALF, ROWS), BF16),
            pltpu.VMEM((2, ZS, OWN, ROWS), BF16),
            pltpu.VMEM((ZS, OWN, ROWS), BF16),
            pltpu.VMEM((ZS, OWN, ROWS), BF16),
            pltpu.VMEM((2 * ZS - 1, OWN, ROWS), BF16),
            pltpu.VMEM((2, OWN, ROWS), BF16),
            pltpu.VMEM((ZS - 1, 2, OWN, ROWS), BF16),
            pltpu.VMEM((OWN, ROWS), BF16),
            pltpu.VMEM((OWN, ROWS), F32),
            pltpu.VMEM((4 * ZS, 128), F32),
            dma((CHUNKS,)),
            dma((BPARTS,)),
            dma((8,)),
            dma,
            dma,
            dma((CHUNKS,)),
            dma((CHUNKS,)),
            dma((CHUNKS,)),
            dma((CHUNKS,)),
            dma((CHUNKS,)),
            dma((CHUNKS,)),
            dma,
            dma,
        ],
        compiler_params=pltpu.CompilerParams(
            collective_id=0, has_side_effects=True, vmem_limit_bytes=56 << 20
        ),
    )(
        candidates,
        train_pts,
        length_rates.reshape(1, DIM),
        kriging_weights.reshape(1, -1),
        component.reshape(1, -1),
        prior_var.reshape(1, CAND),
        factor_panel,
        earlier_solution,
        diag_inverse,
        coupling,
    )
    mean, variance, gradient = [
        pltpu.with_memory_space_constraint(value, pltpu.VMEM) for value in (mean, variance, gradient)
    ]
    whole = pl.BlockSpec(memory_space=pltpu.VMEM)
    mean, variance, gradient = pl.pallas_call(
        deliver, out_shape=shapes, in_specs=[whole] * 3, out_specs=[whole] * 3
    )(mean, variance, gradient)
    return mean.reshape(CAND), variance.reshape(CAND), gradient


def solution(mesh):
    return jax.shard_map(
        shards,
        mesh=mesh,
        in_specs=(
            P(None, "col"),
            P(None, "col"),
            P(),
            P("col"),
            P("col"),
            P("col"),
            P(None, "row"),
            P("row", "col"),
            P(),
            P(),
        ),
        out_specs=(P("col"), P("col"), P(None, "col")),
        check_vma=False,
    )
```

```python
import jax
import jax.numpy as jnp
from jax import lax
from jax.experimental import pallas as pl
from jax.experimental.pallas import tpu as pltpu
from jax.sharding import PartitionSpec as P

MESH = pl.DeviceIdType.MESH
F32 = jnp.float32
BF16 = jnp.bfloat16
NT = (((1,), (1,)), ((), ()))

ROWS = 1024
CAND = 512
DEPTH = 3072
DIM = 32
PARTS = 1
MEET = 1
GIVE = 3
SUMS = ((), (), (0, 1), (2,), (3,))
SIZES = (256, 256, 256, 256)
KINDS = "baad"
ORDER = (1, 2, 0)
HALF = CAND // 2
QUARTER = CAND // 4
OWN = CAND // 32
ZS = 8
CHUNKS = len(SIZES)
STARTS = tuple(sum(SIZES[:c]) for c in range(CHUNKS))
TURNS = (4, 3, 5, 2, 6, 1, 7, 0)
BPARTS = 4


def remote(src, dst, send_sem, recv_sem, **where):
    return pltpu.make_async_remote_copy(
        src_ref=src,
        dst_ref=dst,
        send_sem=send_sem,
        recv_sem=recv_sem,
        device_id=where,
        device_id_type=MESH,
    )


def split(value):
    one = value.astype(BF16)
    rest = value - one.astype(F32)
    two = rest.astype(BF16)
    return [one, two, (rest - two.astype(F32)).astype(BF16)]


def floats(terms):
    return [term.astype(F32) for term in terms]


def kernel(
    cand_hbm,
    points_hbm,
    rates_hbm,
    weights_hbm,
    component_hbm,
    prior_hbm,
    panel_hbm,
    earlier_hbm,
    diag_hbm,
    coupling_hbm,
    mean_ref,
    variance_ref,
    gradient_ref,
    panel,
    earlier,
    diag,
    coupling,
    cand,
    rates,
    prior,
    component,
    pack,
    packs,
    left,
    right,
    by_selector,
    by_points,
    part,
    core_in,
    pair,
    pair_in,
    plane,
    z_in,
    both,
    both_in,
    plane_in,
    own_cross,
    sums,
    panel_sem,
    earlier_sem,
    small_sem,
    pack_send,
    pack_recv,
    core_send,
    core_recv,
    pair_send,
    pair_recv,
    z_send,
    z_recv,
    sums_send,
    sums_recv,
):
    def rows_of(c):
        return pl.ds(STARTS[c], SIZES[c])

    panel_in = [
        pltpu.make_async_copy(
            panel_hbm.at[rows_of(c)], panel.at[rows_of(c)], panel_sem.at[c]
        )
        for c in range(CHUNKS)
    ]
    deep = DEPTH // BPARTS
    earlier_in = [
        pltpu.make_async_copy(
            earlier_hbm.at[pl.ds(i * deep, deep)], earlier.at[pl.ds(i * deep, deep)], earlier_sem.at[i]
        )
        for i in range(BPARTS)
    ]
    panel_in[0].start()
    for copy in earlier_in[: BPARTS // 2]:
        copy.start()

    row = lax.axis_index("row")
    col = lax.axis_index("col")
    core = lax.rem(row, 2)
    z = lax.rem(row // 2, ZS)
    x = row // (2 * ZS)

    half = lax.rem(core + x + z // 4, 2)
    place = (half * 2 + x) * ZS + z
    others = [lax.rem(z + turn, ZS) for turn in TURNS]
    firsts = (16 * x, 16 * (1 - x))
    holds = [lax.rem(half + x + other // 4, 2) for other in others]
    mates = (
        [firsts[0] + 2 * other + hold for other, hold in zip(others, holds)],
        [firsts[1] + 2 * other + 1 - hold for other, hold in zip(others, holds)],
    )
    sibling = 2 * (row // 2) + 1 - core
    y = lax.rem(col, 4)
    beside = firsts[1] + 2 * z + core
    columns = [{"row": beside, "col": 4 - (col - y) + lax.rem(y + turn, 4)} for turn in (2, 1, 3, 0)]
    columns += [{"row": row, "col": col - y + lax.rem(y + turn, 4)} for turn in (2, 1, 3)]
    across = mates[1][ZS - 1]

    barrier = pltpu.get_barrier_semaphore()

    small_in = [
        pltpu.make_async_copy(points_hbm, pack.at[pl.ds(0, DIM)], small_sem.at[0]),
        pltpu.make_async_copy(weights_hbm, pack.at[pl.ds(DIM, 1)], small_sem.at[1]),
        pltpu.make_async_copy(component_hbm, component, small_sem.at[2]),
        pltpu.make_async_copy(cand_hbm, cand, small_sem.at[3]),
        pltpu.make_async_copy(rates_hbm, rates, small_sem.at[4]),
        pltpu.make_async_copy(prior_hbm, prior, small_sem.at[5]),
        pltpu.make_async_copy(diag_hbm, diag, small_sem.at[6]),
        pltpu.make_async_copy(coupling_hbm, coupling, small_sem.at[7]),
    ]

    def greet():
        for device in columns:
            pl.semaphore_signal(barrier, inc=1, device_id=device, device_id_type=MESH)
        for at in mates[1][:2] + mates[0][: ZS - 1] + mates[1][2:] + [sibling]:
            pl.semaphore_signal(barrier, inc=1, device_id={"row": at}, device_id_type=MESH)

    greet()
    for copy in earlier_in[BPARTS // 2 :]:
        copy.start()
    for copy in small_in[:6]:
        copy.start()
    panel_in[0].wait()
    for copy in earlier_in[: BPARTS // 2]:
        copy.wait()
    panel_in[1].start()

    core_copies = [
        remote(
            part.at[pl.ds(pl.multiple_of((1 - half) * HALF, HALF), HALF), rows_of(c)],
            core_in.at[:, rows_of(c)],
            core_send.at[c],
            core_recv.at[c],
            row=sibling,
        )
        for c in range(CHUNKS)
    ]

    def pair_copy(c):
        if KINDS[c] == "b":
            return remote(
                both.at[1 - x, :, rows_of(c)],
                plane_in.at[:, rows_of(c)],
                pair_send.at[c],
                pair_recv.at[c],
                row=across,
            )
        return remote(
            pair.at[1 - x, :, :, rows_of(c)],
            pair_in.at[:, :, rows_of(c)],
            pair_send.at[c],
            pair_recv.at[c],
            row=across,
        )

    def z_copies(c):
        if KINDS[c] == "b":
            ref = both_in.at[:, :, :, rows_of(c)]
        else:
            ref = z_in.at[pl.ds(0, 15 if KINDS[c] == "d" else 7), :, rows_of(c)]
        return remote(ref, ref, z_send.at[c], z_recv.at[c], row=row)

    def core_sum(c):
        core_copies[c].wait_recv()
        mine = part[pl.ds(pl.multiple_of(half * HALF, HALF), HALF), rows_of(c)].astype(F32)
        total = (mine + core_in[:, rows_of(c)].astype(F32)).astype(BF16)
        pair[:, :, :, rows_of(c)] = total.reshape(2, ZS, OWN, SIZES[c])
        if KINDS[c] == "a":
            pair_copy(c).start()
        elif KINDS[c] == "b":
            for i in range(ZS - 1):
                remote(
                    pair.at[:, others[i], :, rows_of(c)],
                    both_in.at[i, :, :, rows_of(c)],
                    z_send.at[c],
                    z_recv.at[c],
                    row=mates[0][i],
                ).start()
        else:
            for i in range(ZS):
                for away in (1, 0):
                    if i < ZS - 1 or away:
                        x_at = 1 - x if away else x
                        remote(
                            pair.at[x_at, others[i], :, rows_of(c)],
                            z_in.at[i + away * (ZS - 1), :, rows_of(c)],
                            z_send.at[c],
                            z_recv.at[c],
                            row=mates[away][i],
                        ).start()

    def pair_sum(c):
        if KINDS[c] == "a":
            pair_copy(c).wait_recv()
            total = pair[x, :, :, rows_of(c)].astype(F32) + pair_in[:, :, rows_of(c)].astype(F32)
            plane[:, :, rows_of(c)] = total.astype(BF16)
            for i in range(ZS - 1):
                remote(
                    plane.at[others[i], :, rows_of(c)],
                    z_in.at[i, :, rows_of(c)],
                    z_send.at[c],
                    z_recv.at[c],
                    row=mates[0][i],
                ).start()
        elif KINDS[c] == "b":
            z_copies(c).wait_recv()
            total = pair[:, z, :, rows_of(c)].astype(F32)
            for i in range(ZS - 1):
                total += both_in[i, :, :, rows_of(c)].astype(F32)
            both[:, :, rows_of(c)] = total.astype(BF16)
            pair_copy(c).start()

    for c in range(CHUNKS):
        if c:
            panel_in[c].wait()
        if c:
            wide = CAND // PARTS
            for i in range(PARTS):
                product = jnp.dot(
                    panel[rows_of(c)], earlier[:, i * wide : (i + 1) * wide], preferred_element_type=F32
                )
                part[pl.ds(i * wide, wide), rows_of(c)] = product.astype(BF16).T
        else:
            product = jnp.zeros((SIZES[0], CAND), F32)
            for i in range(0, BPARTS, BPARTS // 2):
                if i:
                    for copy in earlier_in[BPARTS // 2 :]:
                        copy.wait()
                    for copy in panel_in[2:] + small_in[6:]:
                        copy.start()
                product += jnp.dot(
                    panel[rows_of(c), pl.ds(i * deep, deep * BPARTS // 2)],
                    earlier[pl.ds(i * deep, deep * BPARTS // 2)],
                    preferred_element_type=F32,
                )
            part[:, rows_of(c)] = product.astype(BF16).T
        if c == 0:
            for copy in small_in[:6]:
                copy.wait()
            pack[pl.ds(DIM + 1, 7)] = jnp.zeros((7, 128), F32)
            pack[pl.ds(DIM + 1, 1)] = component[...].astype(F32)
            packs[pl.ds(col, 1)] = pack[...][None]
        if c == MEET:
            pl.semaphore_wait(barrier, 15 + 7 + 1)
            for ready in range(MEET):
                core_copies[ready].start()
        if c >= MEET:
            core_copies[c].start()
        for ready in SUMS[c]:
            core_sum(ready)
        if c == GIVE:
            for device in columns:
                remote(pack, packs.at[col], pack_send, pack_recv, **device).start()
    for ready in SUMS[CHUNKS]:
        core_sum(ready)

    for c in ORDER:
        pair_sum(c)

    packs_moved = remote(
        packs.at[pl.ds(0, 7)], packs.at[pl.ds(0, 7)], pack_send, pack_recv, col=col
    )
    packs_moved.wait_recv()
    lane = lax.broadcasted_iota(jnp.int32, (DIM, DIM), 1)
    level = lax.broadcasted_iota(jnp.int32, (DIM, DIM), 0)
    rate = jnp.sum(jnp.where(lane == level, rates[...], 0.0), axis=1, keepdims=True)
    points = jnp.concatenate([packs[j, :DIM] for j in range(8)], axis=1)
    weights = jnp.concatenate([packs[j, DIM : DIM + 1] for j in range(8)], axis=1)
    kinds = jnp.concatenate([packs[j, DIM + 1 : DIM + 2] for j in range(8)], axis=1)
    scaled = points * rate
    levels = lax.broadcasted_iota(jnp.int32, (DIM, ROWS), 0)
    selector = jnp.where(kinds == (levels + 1).astype(F32), rate, 0.0)
    offset = jnp.where(kinds == 0.0, 1.0, 0.0) - jnp.sum(selector * points, axis=0, keepdims=True)
    point_norm = -0.5 * jnp.sum(scaled * points, axis=0, keepdims=True)
    spread = cand[...]
    cand_norm = -0.5 * jnp.sum(rate * spread * spread, axis=0, keepdims=True)

    def rows_in(shape, first, second):
        at = lax.broadcasted_iota(jnp.int32, shape, 0)
        result = jnp.zeros(shape, F32)
        for i, row_value in enumerate(first + second):
            result = jnp.where(at == i, row_value, result)
        return result.astype(BF16)

    def right_side(factor, first, second):
        one, two, three = split(factor)
        return jnp.concatenate(
            [one, two, one, three, two, one, rows_in((DIM, ROWS), first, second)], axis=0
        )

    ones = [1.0, 1.0, 1.0]
    right[:, :ROWS] = right_side(scaled, floats(split(point_norm)), ones)
    right[:, ROWS:] = right_side(selector, floats(split(offset)), [0.0, 0.0, 0.0])
    one, two, three = split(spread)
    left[:, : 7 * DIM] = jnp.concatenate(
        [one, one, two, one, two, three, rows_in((DIM, CAND), ones, floats(split(cand_norm)))],
        axis=0,
    ).T
    by_selector[...] = jnp.concatenate(split(selector * weights)[:2], axis=0)
    by_points[: 2 * DIM] = jnp.concatenate(split(points * weights)[:2], axis=0)
    by_points[2 * DIM :] = rows_in((DIM, ROWS), floats(split(weights)), [])

    def assemble(some):
        both = jnp.dot(some, right[...], preferred_element_type=F32)
        near = jnp.exp(both[:, :ROWS])
        return near, near * both[:, ROWS:]

    own_cross[...] = assemble(
        left[pl.ds(pl.multiple_of(place * OWN, OWN), OWN), : 7 * DIM]
    )[1]

    def residual(c):
        if KINDS[c] == "b":
            pair_copy(c).wait_recv()
            total = both[x, :, rows_of(c)].astype(F32) + plane_in[:, rows_of(c)].astype(F32)
        else:
            z_copies(c).wait_recv()
            total = pair[x, z, :, rows_of(c)] if KINDS[c] == "d" else plane[z, :, rows_of(c)]
            total = total.astype(F32)
            for i in range(15 if KINDS[c] == "d" else 7):
                total += z_in[i, :, rows_of(c)].astype(F32)
        return (own_cross[:, rows_of(c)] - total).astype(BF16)

    def nt(a, b):
        return lax.dot_general(a, b, NT, preferred_element_type=F32)

    small_in[6].wait()
    small_in[7].wait()
    first_rhs = jnp.concatenate([residual(c) for c in range(CHUNKS) if STARTS[c] < 512], axis=1)
    block_one = nt(first_rhs, diag[0]).astype(BF16)
    coupled = nt(block_one, coupling[...])
    one = block_one.astype(F32)
    squares = jnp.sum(one * one, axis=1, keepdims=True)
    second = jnp.concatenate([residual(c) for c in range(CHUNKS) if STARTS[c] >= 512], axis=1)
    second_rhs = (second.astype(F32) - coupled).astype(BF16)
    two = nt(second_rhs, diag[1]).astype(BF16).astype(F32)
    squares += jnp.sum(two * two, axis=1, keepdims=True)
    lane = lax.broadcasted_iota(jnp.int32, (OWN, QUARTER), 1)
    number = lax.broadcasted_iota(jnp.int32, (OWN, QUARTER), 0)
    sums[pl.ds(place, 1)] = jnp.sum(
        jnp.where(lane == number + z * OWN, squares, 0.0), axis=0, keepdims=True
    )

    for i in range(ZS):
        for first in firsts[::-1]:
            for at in (1 - core, core):
                if i < ZS - 1 or first is not firsts[0] or at is not core:
                    remote(
                        sums.at[pl.ds(place, 1)],
                        sums.at[pl.ds(place, 1)],
                        sums_send,
                        sums_recv,
                        row=first + 2 * others[i] + at,
                    ).start()

    for q in range(4):
        some = pl.ds(q * QUARTER, QUARTER)
        near, cross = assemble(left[some, : 7 * DIM])
        near_one, near_two, _ = split(near)
        cross_one, cross_two, _ = split(cross)
        by_near = (nt(near_one, by_selector[...]) + nt(near_two, by_selector[...])).T
        by_cross = (nt(cross_one, by_points[...]) + nt(cross_two, by_points[...])).T
        mean = jnp.sum(by_cross[2 * DIM :], axis=0, keepdims=True)
        mean_ref[:, some] = mean
        gradient_ref[:, some] = (by_near[:DIM] + by_near[DIM:]) - rate * (
            cand[:, some] * mean - (by_cross[:DIM] + by_cross[DIM : 2 * DIM])
        )

    packs_moved.wait_send()
    for c in range(CHUNKS):
        core_copies[c].wait_send()
        z_copies(c).wait_send()
        if KINDS[c] != "d":
            pair_copy(c).wait_send()

    remote(
        sums.at[pl.ds(0, 4 * ZS - 1)], sums.at[pl.ds(0, 4 * ZS - 1)], sums_send, sums_recv, row=row
    ).wait()
    for q in range(4):
        variance_ref[:, pl.ds(q * QUARTER, QUARTER)] = prior[
            :, pl.ds(q * QUARTER, QUARTER)
        ] - jnp.sum(sums[pl.ds(q * ZS, ZS)], axis=0, keepdims=True)


def deliver(mean, variance, gradient, mean_out, variance_out, gradient_out):
    mean_out[...] = mean[...]
    variance_out[...] = variance[...]
    gradient_out[...] = gradient[...]


def shards(
    candidates,
    train_pts,
    length_rates,
    kriging_weights,
    component,
    prior_var,
    factor_panel,
    earlier_solution,
    diag_inverse,
    coupling,
):
    dma = pltpu.SemaphoreType.DMA
    shapes = (
        jax.ShapeDtypeStruct((1, CAND), F32),
        jax.ShapeDtypeStruct((1, CAND), F32),
        jax.ShapeDtypeStruct((DIM, CAND), F32),
    )
    mean, variance, gradient = pl.pallas_call(
        kernel,
        out_shape=tuple(pltpu.VMEM(shape.shape, F32) for shape in shapes),
        in_specs=[pl.BlockSpec(memory_space=pltpu.HBM)] * 10,
        out_specs=[pl.BlockSpec(memory_space=pltpu.VMEM)] * 3,
        scratch_shapes=[
            pltpu.VMEM((ROWS, DEPTH), BF16),
            pltpu.VMEM((DEPTH, CAND), BF16),
            pltpu.VMEM((2, 512, 512), BF16),
            pltpu.VMEM((512, 512), BF16),
            pltpu.VMEM((DIM, CAND), F32),
            pltpu.VMEM((1, DIM), F32),
            pltpu.VMEM((1, CAND), F32),
            pltpu.VMEM((1, 128), jnp.int32),
            pltpu.VMEM((DIM + 8, 128), F32),
            pltpu.VMEM((8, DIM + 8, 128), F32),
            pltpu.VMEM((CAND, 8 * DIM), BF16),
            pltpu.VMEM((7 * DIM, 2 * ROWS), BF16),
            pltpu.VMEM((2 * DIM, ROWS), BF16),
            pltpu.VMEM((3 * DIM, ROWS), BF16),
            pltpu.VMEM((CAND, ROWS), BF16),
            pltpu.VMEM((HALF, ROWS), BF16),
            pltpu.VMEM((2, ZS, OWN, ROWS), BF16),
            pltpu.VMEM((ZS, OWN, ROWS), BF16),
            pltpu.VMEM((ZS, OWN, ROWS), BF16),
            pltpu.VMEM((2 * ZS - 1, OWN, ROWS), BF16),
            pltpu.VMEM((2, OWN, ROWS), BF16),
            pltpu.VMEM((ZS - 1, 2, OWN, ROWS), BF16),
            pltpu.VMEM((OWN, ROWS), BF16),
            pltpu.VMEM((OWN, ROWS), F32),
            pltpu.VMEM((4 * ZS, 128), F32),
            dma((CHUNKS,)),
            dma((BPARTS,)),
            dma((8,)),
            dma,
            dma,
            dma((CHUNKS,)),
            dma((CHUNKS,)),
            dma((CHUNKS,)),
            dma((CHUNKS,)),
            dma((CHUNKS,)),
            dma((CHUNKS,)),
            dma,
            dma,
        ],
        compiler_params=pltpu.CompilerParams(
            collective_id=0, has_side_effects=True, vmem_limit_bytes=56 << 20
        ),
    )(
        candidates,
        train_pts,
        length_rates.reshape(1, DIM),
        kriging_weights.reshape(1, -1),
        component.reshape(1, -1),
        prior_var.reshape(1, CAND),
        factor_panel,
        earlier_solution,
        diag_inverse,
        coupling,
    )
    mean, variance, gradient = [
        pltpu.with_memory_space_constraint(value, pltpu.VMEM) for value in (mean, variance, gradient)
    ]
    whole = pl.BlockSpec(memory_space=pltpu.VMEM)
    mean, variance, gradient = pl.pallas_call(
        deliver, out_shape=shapes, in_specs=[whole] * 3, out_specs=[whole] * 3
    )(mean, variance, gradient)
    return mean.reshape(CAND), variance.reshape(CAND), gradient


def solution(mesh):
    return jax.shard_map(
        shards,
        mesh=mesh,
        in_specs=(
            P(None, "col"),
            P(None, "col"),
            P(),
            P("col"),
            P("col"),
            P("col"),
            P(None, "row"),
            P("row", "col"),
            P(),
            P(),
        ),
        out_specs=(P("col"), P("col"), P(None, "col")),
        check_vma=False,
    )
```

```python
import jax
import jax.numpy as jnp
from jax import lax
from jax.experimental import pallas as pl
from jax.experimental.pallas import tpu as pltpu
from jax.sharding import PartitionSpec as P

MESH = pl.DeviceIdType.MESH
F32 = jnp.float32
BF16 = jnp.bfloat16
NT = (((1,), (1,)), ((), ()))

ROWS = 1024
CAND = 512
DEPTH = 3072
DIM = 32
PARTS = 1
MEET = 1
GIVE = 3
SUMS = ((), (), (0, 1), (2,), (3,))
SIZES = (256, 256, 256, 256)
KINDS = "baad"
ORDER = (1, 2, 0)
HALF = CAND // 2
QUARTER = CAND // 4
OWN = CAND // 32
ZS = 8
CHUNKS = len(SIZES)
STARTS = tuple(sum(SIZES[:c]) for c in range(CHUNKS))
TURNS = (4, 3, 5, 2, 6, 1, 7, 0)
BPARTS = 4


def remote(src, dst, send_sem, recv_sem, **where):
    return pltpu.make_async_remote_copy(
        src_ref=src,
        dst_ref=dst,
        send_sem=send_sem,
        recv_sem=recv_sem,
        device_id=where,
        device_id_type=MESH,
    )


def split(value):
    one = value.astype(BF16)
    rest = value - one.astype(F32)
    two = rest.astype(BF16)
    return [one, two, (rest - two.astype(F32)).astype(BF16)]


def floats(terms):
    return [term.astype(F32) for term in terms]


def kernel(
    cand_hbm,
    points_hbm,
    rates_hbm,
    weights_hbm,
    component_hbm,
    prior_hbm,
    panel_hbm,
    earlier_hbm,
    diag_hbm,
    coupling_hbm,
    mean_ref,
    variance_ref,
    gradient_ref,
    panel,
    earlier,
    diag,
    coupling,
    cand,
    rates,
    prior,
    component,
    pack,
    packs,
    left,
    right,
    by_selector,
    by_points,
    part,
    core_in,
    pair,
    pair_in,
    plane,
    z_in,
    both,
    both_in,
    plane_in,
    own_cross,
    sums,
    panel_sem,
    earlier_sem,
    small_sem,
    pack_send,
    pack_recv,
    core_send,
    core_recv,
    pair_send,
    pair_recv,
    z_send,
    z_recv,
    sums_send,
    sums_recv,
):
    def rows_of(c):
        return pl.ds(STARTS[c], SIZES[c])

    panel_in = [
        pltpu.make_async_copy(
            panel_hbm.at[rows_of(c)], panel.at[rows_of(c)], panel_sem.at[c]
        )
        for c in range(CHUNKS)
    ]
    deep = DEPTH // BPARTS
    earlier_in = [
        pltpu.make_async_copy(
            earlier_hbm.at[pl.ds(i * deep, deep)], earlier.at[pl.ds(i * deep, deep)], earlier_sem.at[i]
        )
        for i in range(BPARTS)
    ]
    panel_in[0].start()
    for copy in earlier_in[: BPARTS // 2]:
        copy.start()

    row = lax.axis_index("row")
    col = lax.axis_index("col")
    core = lax.rem(row, 2)
    z = lax.rem(row // 2, ZS)
    x = row // (2 * ZS)

    half = lax.rem(core + x + z // 4, 2)
    place = (half * 2 + x) * ZS + z
    others = [lax.rem(z + turn, ZS) for turn in TURNS]
    firsts = (16 * x, 16 * (1 - x))
    holds = [lax.rem(half + x + other // 4, 2) for other in others]
    mates = (
        [firsts[0] + 2 * other + hold for other, hold in zip(others, holds)],
        [firsts[1] + 2 * other + 1 - hold for other, hold in zip(others, holds)],
    )
    sibling = 2 * (row // 2) + 1 - core
    y = lax.rem(col, 4)
    beside = firsts[1] + 2 * z + core
    columns = [{"row": beside, "col": 4 - (col - y) + lax.rem(y + turn, 4)} for turn in (2, 1, 3, 0)]
    columns += [{"row": row, "col": col - y + lax.rem(y + turn, 4)} for turn in (2, 1, 3)]
    across = mates[1][ZS - 1]

    barrier = pltpu.get_barrier_semaphore()

    small_in = [
        pltpu.make_async_copy(points_hbm, pack.at[pl.ds(0, DIM)], small_sem.at[0]),
        pltpu.make_async_copy(weights_hbm, pack.at[pl.ds(DIM, 1)], small_sem.at[1]),
        pltpu.make_async_copy(component_hbm, component, small_sem.at[2]),
        pltpu.make_async_copy(cand_hbm, cand, small_sem.at[3]),
        pltpu.make_async_copy(rates_hbm, rates, small_sem.at[4]),
        pltpu.make_async_copy(prior_hbm, prior, small_sem.at[5]),
        pltpu.make_async_copy(diag_hbm, diag, small_sem.at[6]),
        pltpu.make_async_copy(coupling_hbm, coupling, small_sem.at[7]),
    ]

    def greet():
        for device in columns:
            pl.semaphore_signal(barrier, inc=1, device_id=device, device_id_type=MESH)
        for at in mates[1][:2] + mates[0][: ZS - 1] + mates[1][2:] + [sibling]:
            pl.semaphore_signal(barrier, inc=1, device_id={"row": at}, device_id_type=MESH)

    greet()
    for copy in earlier_in[BPARTS // 2 :]:
        copy.start()
    for copy in small_in[:6]:
        copy.start()
    panel_in[0].wait()
    for copy in earlier_in[: BPARTS // 2]:
        copy.wait()
    panel_in[1].start()

    core_copies = [
        remote(
            part.at[pl.ds(pl.multiple_of((1 - half) * HALF, HALF), HALF), rows_of(c)],
            core_in.at[:, rows_of(c)],
            core_send.at[c],
            core_recv.at[c],
            row=sibling,
        )
        for c in range(CHUNKS)
    ]

    def pair_copy(c):
        if KINDS[c] == "b":
            return remote(
                both.at[1 - x, :, rows_of(c)],
                plane_in.at[:, rows_of(c)],
                pair_send.at[c],
                pair_recv.at[c],
                row=across,
            )
        return remote(
            pair.at[1 - x, :, :, rows_of(c)],
            pair_in.at[:, :, rows_of(c)],
            pair_send.at[c],
            pair_recv.at[c],
            row=across,
        )

    def z_copies(c):
        if KINDS[c] == "b":
            ref = both_in.at[:, :, :, rows_of(c)]
        else:
            ref = z_in.at[pl.ds(0, 15 if KINDS[c] == "d" else 7), :, rows_of(c)]
        return remote(ref, ref, z_send.at[c], z_recv.at[c], row=row)

    def core_sum(c):
        core_copies[c].wait_recv()
        mine = part[pl.ds(pl.multiple_of(half * HALF, HALF), HALF), rows_of(c)].astype(F32)
        total = (mine + core_in[:, rows_of(c)].astype(F32)).astype(BF16)
        pair[:, :, :, rows_of(c)] = total.reshape(2, ZS, OWN, SIZES[c])
        if KINDS[c] == "a":
            pair_copy(c).start()
        elif KINDS[c] == "b":
            for i in range(ZS - 1):
                remote(
                    pair.at[:, others[i], :, rows_of(c)],
                    both_in.at[i, :, :, rows_of(c)],
                    z_send.at[c],
                    z_recv.at[c],
                    row=mates[0][i],
                ).start()
        else:
            for i in range(ZS):
                for away in (1, 0):
                    if i < ZS - 1 or away:
                        x_at = 1 - x if away else x
                        remote(
                            pair.at[x_at, others[i], :, rows_of(c)],
                            z_in.at[i + away * (ZS - 1), :, rows_of(c)],
                            z_send.at[c],
                            z_recv.at[c],
                            row=mates[away][i],
                        ).start()

    def pair_sum(c):
        if KINDS[c] == "a":
            pair_copy(c).wait_recv()
            total = pair[x, :, :, rows_of(c)].astype(F32) + pair_in[:, :, rows_of(c)].astype(F32)
            plane[:, :, rows_of(c)] = total.astype(BF16)
            for i in range(ZS - 1):
                remote(
                    plane.at[others[i], :, rows_of(c)],
                    z_in.at[i, :, rows_of(c)],
                    z_send.at[c],
                    z_recv.at[c],
                    row=mates[0][i],
                ).start()
        elif KINDS[c] == "b":
            z_copies(c).wait_recv()
            total = pair[:, z, :, rows_of(c)].astype(F32)
            for i in range(ZS - 1):
                total += both_in[i, :, :, rows_of(c)].astype(F32)
            both[:, :, rows_of(c)] = total.astype(BF16)
            pair_copy(c).start()

    for c in range(CHUNKS):
        if c:
            panel_in[c].wait()
        if c:
            wide = CAND // PARTS
            for i in range(PARTS):
                product = jnp.dot(
                    panel[rows_of(c)], earlier[:, i * wide : (i + 1) * wide], preferred_element_type=F32
                )
                part[pl.ds(i * wide, wide), rows_of(c)] = product.astype(BF16).T
        else:
            product = jnp.zeros((SIZES[0], CAND), F32)
            for i in range(0, BPARTS, BPARTS // 2):
                if i:
                    for copy in earlier_in[BPARTS // 2 :]:
                        copy.wait()
                    for copy in panel_in[2:] + small_in[6:]:
                        copy.start()
                product += jnp.dot(
                    panel[rows_of(c), pl.ds(i * deep, deep * BPARTS // 2)],
                    earlier[pl.ds(i * deep, deep * BPARTS // 2)],
                    preferred_element_type=F32,
                )
            part[:, rows_of(c)] = product.astype(BF16).T
        if c == MEET:
            pl.semaphore_wait(barrier, 15 + 7 + 1)
            for ready in range(MEET):
                core_copies[ready].start()
        if c >= MEET:
            core_copies[c].start()
        for ready in SUMS[c]:
            core_sum(ready)
        if c == GIVE:
            for copy in small_in[:6]:
                copy.wait()
            pack[pl.ds(DIM + 1, 7)] = jnp.zeros((7, 128), F32)
            pack[pl.ds(DIM + 1, 1)] = component[...].astype(F32)
            packs[pl.ds(col, 1)] = pack[...][None]
            for device in columns:
                remote(pack, packs.at[col], pack_send, pack_recv, **device).start()
    for ready in SUMS[CHUNKS]:
        core_sum(ready)

    for c in ORDER:
        pair_sum(c)

    packs_moved = remote(
        packs.at[pl.ds(0, 7)], packs.at[pl.ds(0, 7)], pack_send, pack_recv, col=col
    )
    packs_moved.wait_recv()
    lane = lax.broadcasted_iota(jnp.int32, (DIM, DIM), 1)
    level = lax.broadcasted_iota(jnp.int32, (DIM, DIM), 0)
    rate = jnp.sum(jnp.where(lane == level, rates[...], 0.0), axis=1, keepdims=True)
    points = jnp.concatenate([packs[j, :DIM] for j in range(8)], axis=1)
    weights = jnp.concatenate([packs[j, DIM : DIM + 1] for j in range(8)], axis=1)
    kinds = jnp.concatenate([packs[j, DIM + 1 : DIM + 2] for j in range(8)], axis=1)
    scaled = points * rate
    levels = lax.broadcasted_iota(jnp.int32, (DIM, ROWS), 0)
    selector = jnp.where(kinds == (levels + 1).astype(F32), rate, 0.0)
    offset = jnp.where(kinds == 0.0, 1.0, 0.0) - jnp.sum(selector * points, axis=0, keepdims=True)
    point_norm = -0.5 * jnp.sum(scaled * points, axis=0, keepdims=True)
    spread = cand[...]
    cand_norm = -0.5 * jnp.sum(rate * spread * spread, axis=0, keepdims=True)

    def rows_in(shape, first, second):
        at = lax.broadcasted_iota(jnp.int32, shape, 0)
        result = jnp.zeros(shape, F32)
        for i, row_value in enumerate(first + second):
            result = jnp.where(at == i, row_value, result)
        return result.astype(BF16)

    def right_side(factor, first, second):
        one, two, three = split(factor)
        return jnp.concatenate(
            [one, two, one, three, two, one, rows_in((DIM, ROWS), first, second)], axis=0
        )

    ones = [1.0, 1.0, 1.0]
    right[:, :ROWS] = right_side(scaled, floats(split(point_norm)), ones)
    right[:, ROWS:] = right_side(selector, floats(split(offset)), [0.0, 0.0, 0.0])
    one, two, three = split(spread)
    left[:, : 7 * DIM] = jnp.concatenate(
        [one, one, two, one, two, three, rows_in((DIM, CAND), ones, floats(split(cand_norm)))],
        axis=0,
    ).T
    by_selector[...] = jnp.concatenate(split(selector * weights)[:2], axis=0)
    by_points[: 2 * DIM] = jnp.concatenate(split(points * weights)[:2], axis=0)
    by_points[2 * DIM :] = rows_in((DIM, ROWS), floats(split(weights)), [])

    def assemble(some):
        both = jnp.dot(some, right[...], preferred_element_type=F32)
        near = jnp.exp(both[:, :ROWS])
        return near, near * both[:, ROWS:]

    own_cross[...] = assemble(
        left[pl.ds(pl.multiple_of(place * OWN, OWN), OWN), : 7 * DIM]
    )[1]

    def residual(c):
        if KINDS[c] == "b":
            pair_copy(c).wait_recv()
            total = both[x, :, rows_of(c)].astype(F32) + plane_in[:, rows_of(c)].astype(F32)
        else:
            z_copies(c).wait_recv()
            total = pair[x, z, :, rows_of(c)] if KINDS[c] == "d" else plane[z, :, rows_of(c)]
            total = total.astype(F32)
            for i in range(15 if KINDS[c] == "d" else 7):
                total += z_in[i, :, rows_of(c)].astype(F32)
        return (own_cross[:, rows_of(c)] - total).astype(BF16)

    def nt(a, b):
        return lax.dot_general(a, b, NT, preferred_element_type=F32)

    small_in[6].wait()
    small_in[7].wait()
    first_rhs = jnp.concatenate([residual(c) for c in range(CHUNKS) if STARTS[c] < 512], axis=1)
    block_one = nt(first_rhs, diag[0]).astype(BF16)
    coupled = nt(block_one, coupling[...])
    one = block_one.astype(F32)
    squares = jnp.sum(one * one, axis=1, keepdims=True)
    second = jnp.concatenate([residual(c) for c in range(CHUNKS) if STARTS[c] >= 512], axis=1)
    second_rhs = (second.astype(F32) - coupled).astype(BF16)
    two = nt(second_rhs, diag[1]).astype(BF16).astype(F32)
    squares += jnp.sum(two * two, axis=1, keepdims=True)
    lane = lax.broadcasted_iota(jnp.int32, (OWN, QUARTER), 1)
    number = lax.broadcasted_iota(jnp.int32, (OWN, QUARTER), 0)
    sums[pl.ds(place, 1)] = jnp.sum(
        jnp.where(lane == number + z * OWN, squares, 0.0), axis=0, keepdims=True
    )

    for i in range(ZS):
        for first in firsts[::-1]:
            for at in (1 - core, core):
                if i < ZS - 1 or first is not firsts[0] or at is not core:
                    remote(
                        sums.at[pl.ds(place, 1)],
                        sums.at[pl.ds(place, 1)],
                        sums_send,
                        sums_recv,
                        row=first + 2 * others[i] + at,
                    ).start()

    for q in range(4):
        some = pl.ds(q * QUARTER, QUARTER)
        near, cross = assemble(left[some, : 7 * DIM])
        near_one, near_two, _ = split(near)
        cross_one, cross_two, _ = split(cross)
        by_near = (nt(near_one, by_selector[...]) + nt(near_two, by_selector[...])).T
        by_cross = (nt(cross_one, by_points[...]) + nt(cross_two, by_points[...])).T
        mean = jnp.sum(by_cross[2 * DIM :], axis=0, keepdims=True)
        mean_ref[:, some] = mean
        gradient_ref[:, some] = (by_near[:DIM] + by_near[DIM:]) - rate * (
            cand[:, some] * mean - (by_cross[:DIM] + by_cross[DIM : 2 * DIM])
        )

    packs_moved.wait_send()
    for c in range(CHUNKS):
        core_copies[c].wait_send()
        z_copies(c).wait_send()
        if KINDS[c] != "d":
            pair_copy(c).wait_send()

    remote(
        sums.at[pl.ds(0, 4 * ZS - 1)], sums.at[pl.ds(0, 4 * ZS - 1)], sums_send, sums_recv, row=row
    ).wait()
    for q in range(4):
        variance_ref[:, pl.ds(q * QUARTER, QUARTER)] = prior[
            :, pl.ds(q * QUARTER, QUARTER)
        ] - jnp.sum(sums[pl.ds(q * ZS, ZS)], axis=0, keepdims=True)


def deliver(mean, variance, gradient, mean_out, variance_out, gradient_out):
    mean_out[...] = mean[...]
    variance_out[...] = variance[...]
    gradient_out[...] = gradient[...]


def shards(
    candidates,
    train_pts,
    length_rates,
    kriging_weights,
    component,
    prior_var,
    factor_panel,
    earlier_solution,
    diag_inverse,
    coupling,
):
    dma = pltpu.SemaphoreType.DMA
    shapes = (
        jax.ShapeDtypeStruct((1, CAND), F32),
        jax.ShapeDtypeStruct((1, CAND), F32),
        jax.ShapeDtypeStruct((DIM, CAND), F32),
    )
    mean, variance, gradient = pl.pallas_call(
        kernel,
        out_shape=tuple(pltpu.VMEM(shape.shape, F32) for shape in shapes),
        in_specs=[pl.BlockSpec(memory_space=pltpu.HBM)] * 10,
        out_specs=[pl.BlockSpec(memory_space=pltpu.VMEM)] * 3,
        scratch_shapes=[
            pltpu.VMEM((ROWS, DEPTH), BF16),
            pltpu.VMEM((DEPTH, CAND), BF16),
            pltpu.VMEM((2, 512, 512), BF16),
            pltpu.VMEM((512, 512), BF16),
            pltpu.VMEM((DIM, CAND), F32),
            pltpu.VMEM((1, DIM), F32),
            pltpu.VMEM((1, CAND), F32),
            pltpu.VMEM((1, 128), jnp.int32),
            pltpu.VMEM((DIM + 8, 128), F32),
            pltpu.VMEM((8, DIM + 8, 128), F32),
            pltpu.VMEM((CAND, 8 * DIM), BF16),
            pltpu.VMEM((7 * DIM, 2 * ROWS), BF16),
            pltpu.VMEM((2 * DIM, ROWS), BF16),
            pltpu.VMEM((3 * DIM, ROWS), BF16),
            pltpu.VMEM((CAND, ROWS), BF16),
            pltpu.VMEM((HALF, ROWS), BF16),
            pltpu.VMEM((2, ZS, OWN, ROWS), BF16),
            pltpu.VMEM((ZS, OWN, ROWS), BF16),
            pltpu.VMEM((ZS, OWN, ROWS), BF16),
            pltpu.VMEM((2 * ZS - 1, OWN, ROWS), BF16),
            pltpu.VMEM((2, OWN, ROWS), BF16),
            pltpu.VMEM((ZS - 1, 2, OWN, ROWS), BF16),
            pltpu.VMEM((OWN, ROWS), BF16),
            pltpu.VMEM((OWN, ROWS), F32),
            pltpu.VMEM((4 * ZS, 128), F32),
            dma((CHUNKS,)),
            dma((BPARTS,)),
            dma((8,)),
            dma,
            dma,
            dma((CHUNKS,)),
            dma((CHUNKS,)),
            dma((CHUNKS,)),
            dma((CHUNKS,)),
            dma((CHUNKS,)),
            dma((CHUNKS,)),
            dma,
            dma,
        ],
        compiler_params=pltpu.CompilerParams(
            collective_id=0, has_side_effects=True, vmem_limit_bytes=56 << 20
        ),
    )(
        candidates,
        train_pts,
        length_rates.reshape(1, DIM),
        kriging_weights.reshape(1, -1),
        component.reshape(1, -1),
        prior_var.reshape(1, CAND),
        factor_panel,
        earlier_solution,
        diag_inverse,
        coupling,
    )
    mean, variance, gradient = [
        pltpu.with_memory_space_constraint(value, pltpu.VMEM) for value in (mean, variance, gradient)
    ]
    whole = pl.BlockSpec(memory_space=pltpu.VMEM)
    mean, variance, gradient = pl.pallas_call(
        deliver, out_shape=shapes, in_specs=[whole] * 3, out_specs=[whole] * 3
    )(mean, variance, gradient)
    return mean.reshape(CAND), variance.reshape(CAND), gradient


def solution(mesh):
    return jax.shard_map(
        shards,
        mesh=mesh,
        in_specs=(
            P(None, "col"),
            P(None, "col"),
            P(),
            P("col"),
            P("col"),
            P("col"),
            P(None, "row"),
            P("row", "col"),
            P(),
            P(),
        ),
        out_specs=(P("col"), P("col"), P(None, "col")),
        check_vma=False,
    )
```
